32 devices in a mesh: parts: 2 (over x), expert: 16 (over z, y, core).
Axes of the slice: x: 2, y: 2, z: 4, core: 2. Of those that a mesh axis runs over, the one named last changes fastest.
Arguments:
- hidden: bfloat16 [512, 2048], P(('parts', 'expert')), parts along dimension 0, may hold values from -6 to 6
- parent: int32 [512], P(('parts', 'expert')), parts along dimension 0, may hold values from 0 to 255, as said below
- expert_ids: int32 [512, 8], P(('parts', 'expert')), parts along dimension 0, may hold values from 0 to 15, all different within a row; in each aligned block of 16 rows (0 to 15, 16 to 31, ...) at most 16 rows name the same one
- route_weight: float32 [512, 8], P(('parts', 'expert')), parts along dimension 0, may hold values from 0.05 to 1
- norm_gain: float32 [2048], replicated, may hold values from 0.1 to 1.9
- w_gate: bfloat16 [16, 2048, 768], P('expert'), may hold values from -0.125 to 0.125
- w_up: bfloat16 [16, 2048, 768], P('expert'), may hold values from -0.125 to 0.125
- w_down: bfloat16 [16, 768, 2048], P('expert'), may hold values from -0.21875 to 0.21875
Outputs:
- layer_out: bfloat16 [512, 2048], P(('parts', 'expert')), parts along dimension 0
The draws below stay inside these ranges and needn't reach their ends.
There are 2 independent parts, one for each index of `parts`. The reference program is written for one: setup_inputs(seed, part) draws one part's arguments, and reference() takes and returns one part's arrays. A program takes and returns all parts, laid end to end along the dimension named above; an argument that names none is the same for every part. Nothing has to cross between parts.
Inputs may be any that keep to these rules, and one draw needn't show every extreme that they name: The parent of a row among the rows 16 * i to 16 * i + 15 lies in the same range or in the range just before it. `expert_ids`: in each aligned block of 16 rows (the rows of one device) no expert is named by more than 16 rows, a bound that some block reaches.
All inputs are finite; a program needn't handle non-finite values.
Results may differ from the reference program's by a relative error of at most 0.0033.
Values may be sent and summed in bfloat16 or wider, within the bound.
A program may use at most 64 MiB of HBM per device.

```python
import math
import jax
import jax.numpy as jnp
import numpy as np
from jax import lax

D = 2048
FF = 768
TOP = 8
ROWS_DEV = 16
EXPERTS = 16
ROWS = 256
CAP = 16
N_EXPERT = 16


def draw_parent(key, part):
    key = jax.random.fold_in(key, 7)
    row_no = jnp.arange(ROWS, dtype=jnp.int32)
    block_no = row_no // ROWS_DEV
    low_end = jnp.maximum(block_no - 1, 0) * ROWS_DEV
    high_end = (block_no + 1) * ROWS_DEV
    raw = jax.random.randint(key, (ROWS,), 0, 1 << 20, dtype=jnp.int32)
    chosen = low_end + raw % (high_end - low_end)
    chosen = jnp.where(row_no == ROWS - 1, ROWS - 1, chosen)
    chosen = jnp.where(row_no == 0, 0, chosen)
    return chosen.astype(jnp.int32)


def block_levels(stream_key, shape, pieces, smallest, high):
    def one(axis_at, shards_of):
        heights = jax.random.uniform(jax.random.fold_in(jax.random.fold_in(stream_key, 6), axis_at), (shards_of,), jnp.float32, smallest / len(pieces), high / len(pieces))
        return jnp.repeat(jnp.exp(heights), shape[axis_at] // shards_of).reshape((-1,) + (1,) * (len(shape) - axis_at - 1))

    gain = one(*pieces[0])
    for cut in pieces[1:]:
        gain = gain * one(*cut)
    return gain


def routed_block(own_key, own, number, rows, number_of, top, reach, lean):
    order = jax.random.permutation(own_key, number_of)
    heavy_load, ordinary = load_shares(number_of, rows * top, reach, lean, True), load_shares(number_of, rows * top, reach, lean, False)
    places = jnp.arange(number_of)

    def named(sizes, offset_by):
        used = int((sizes > 0).sum())
        fixed = max(1, used // 4)
        passed = fixed + (places - fixed + offset_by * (used - fixed)) % max(1, number_of - fixed)
        return jnp.zeros((number_of,), jnp.int32).at[order[jnp.where(places < fixed, places, passed)]].set(jnp.asarray(sizes, jnp.int32))

    sizes = jnp.where(number % 4 == 0, named(heavy_load, number // 4), named(ordinary, number - number // 4 - 1))
    mixed = jax.random.permutation(jax.random.fold_in(own, 3), number_of)
    giver, taker = mixed[0:number_of // 2 * 2:2], mixed[1:number_of // 2 * 2:2]
    margin = jnp.minimum(sizes[giver] - 1, reach - sizes[taker]) // 2
    margin = jnp.where((giver == order[0]) | (taker == order[0]) | (sizes[taker] == 0), 0, jnp.maximum(margin, 0))
    passed = jax.random.randint(jax.random.fold_in(own, 4), (number_of // 2,), 0, 1 << 20) % (margin + 1)
    sizes = sizes.at[giver].add(-passed).at[taker].add(passed)
    labels = jnp.searchsorted(jnp.cumsum(sizes), jnp.arange(rows * top), side="right").astype(jnp.int32)
    listing = labels.reshape(top, rows).T
    listing = listing[jax.random.permutation(jax.random.fold_in(own, 1), rows)]
    offset_by = jax.random.randint(jax.random.fold_in(own, 2), (rows, 1), 0, top)
    return jnp.take_along_axis(listing, (jnp.arange(top)[None, :] + offset_by) % top, axis=1)


def load_shares(count, total, bound, slope, full):
    weights = [(1 << 20) // math.isqrt(grade ** slope) + 1 for grade in range(1, count + 1)]
    largest = bound if full else min(bound, max(-(-total // count), total * weights[0] // sum(weights)))
    least = 1 if total - largest >= count - 1 else 0
    holding, spare = [largest] + [least] * (count - 1), total - largest - least * (count - 1)
    while spare > 0:
        candidates = [i for i in range(1, count) if holding[i] < largest] or [i for i in range(1, count) if holding[i] < bound]
        whole, budget = sum([weights[i] for i in candidates]), spare
        for i in candidates:
            more = min(bound - holding[i], max(1, budget * weights[i] // whole), spare)
            holding[i] = holding[i] + more
            spare = spare - more
    return np.array(holding)


def centred(key, extent, spread, reach, split=(), held_as=jnp.bfloat16):
    values = spread * jax.random.normal(key, extent, jnp.float32)
    if split:
        values = values * block_levels(key, extent, split, -0.22, 0.18)
    return jnp.clip(values, -reach, reach).astype(held_as)


def setup_inputs(seed: int = 0, part: int = 0) -> dict:
    seeds = jax.random.split(jax.random.key(seed), 9)
    part_splits = jax.random.split(jax.random.fold_in(seeds[8], part), 9)
    hidden = centred(part_splits[0], (ROWS, D), 1.0, 6.0, ((0, 16),))
    parent = draw_parent(jax.random.fold_in(jax.random.fold_in(seeds[8], part), 71), part)
    expert_ids_keys = jax.random.split(jax.random.fold_in(part_splits[2], 1), ROWS // ROWS_DEV)
    expert_ids_turns = jax.random.permutation(jax.random.fold_in(part_splits[2], 3), ROWS // ROWS_DEV)
    expert_ids = jax.vmap(lambda own, number: routed_block(jax.random.fold_in(part_splits[2], 2), own, number, ROWS_DEV, EXPERTS, TOP, CAP, 2))(expert_ids_keys, expert_ids_turns).reshape((ROWS, TOP))
    route_weight = jnp.clip(jnp.exp(math.log(1.0) - 2.9957323 * jax.random.uniform(part_splits[3], (ROWS, TOP), jnp.float32) ** block_levels(part_splits[3], (ROWS, TOP), ((0, 16),), -0.2, 0.2)), 0.05, 1.0)
    norm_gain = jnp.clip(1.0 + 0.18 * jax.random.normal(seeds[4], (D,), jnp.float32), 0.1, 1.9)
    w_gate = centred(seeds[5], (EXPERTS, D, FF), D ** -0.5, 0.125, ((0, 16),))
    w_up = centred(seeds[6], (EXPERTS, D, FF), D ** -0.5, 0.125, ((0, 16),))
    w_down = centred(seeds[7], (EXPERTS, FF, D), FF ** -0.5, 0.21875, ((0, 16),))
    return {"hidden": hidden, "parent": parent, "expert_ids": expert_ids, "route_weight": route_weight, "norm_gain": norm_gain, "w_gate": w_gate, "w_up": w_up, "w_down": w_down}


def reference(hidden, parent, expert_ids, route_weight, norm_gain, w_gate, w_up, w_down):
    forked = jnp.take(hidden, parent, axis=0)
    forked_f = forked.astype(jnp.float32)
    scale_row = lax.rsqrt(lax.optimization_barrier(jnp.mean(forked_f * forked_f, axis=-1, keepdims=True)) + 1e-06)
    normed = (forked_f * scale_row * norm_gain).astype(jnp.bfloat16)
    share = route_weight / lax.optimization_barrier(jnp.sum(route_weight, axis=-1, keepdims=True))
    flat_ids = expert_ids.reshape(-1)
    flat_share = share.reshape(-1)
    most_slots = N_EXPERT * CAP

    def one_expert(total, expert_no):
        hit = flat_ids == expert_no
        hit_count = jnp.sum(hit.astype(jnp.int32))
        picked = jnp.nonzero(hit, size=most_slots, fill_value=0)[0].astype(jnp.int32)
        row_pick = (picked // TOP).astype(jnp.int32)
        inputs = jnp.take(normed, row_pick, axis=0)
        gate_val = jnp.dot(inputs, w_gate[expert_no], preferred_element_type=jnp.float32)
        up_val = jnp.dot(inputs, w_up[expert_no], preferred_element_type=jnp.float32)
        inner = (jax.nn.silu(gate_val) * up_val).astype(jnp.bfloat16)
        result = jnp.dot(inner, w_down[expert_no], preferred_element_type=jnp.float32).astype(jnp.bfloat16)
        live = jnp.arange(most_slots) < hit_count
        weights = jnp.where(live, jnp.take(flat_share, picked), jnp.zeros((), jnp.float32))
        total = total.at[row_pick].add(weights[:, None] * result.astype(jnp.float32))
        return (total, None)
    start_total = jnp.zeros((ROWS, D), jnp.float32)
    total, unused = lax.scan(one_expert, start_total, jnp.arange(EXPERTS, dtype=jnp.int32))
    return (forked_f + total).astype(jnp.bfloat16)
```

```python
import functools

import jax
import jax.numpy as jnp
from jax import lax
from jax.experimental import pallas as pl
from jax.experimental.pallas import tpu as pltpu
from jax.sharding import PartitionSpec as P

MESH = pl.DeviceIdType.MESH
GATHER_CHUNKS = 2
RETURN_CHUNKS = 2
LANES = 128


def dense_kernel(
    parent_ref, hidden_ref, ids_ref, weight_ref, gain_ref, gate_hbm, up_hbm, down_hbm,
    out_ref,
    *scratch,
    experts, zs,
):
    gc, rc = GATHER_CHUNKS, RETURN_CHUNKS
    scratch = list(scratch)
    rows_in = [scratch.pop(0) for _ in range(gc)]
    (gate_w, up_w, down_w, gate_acc, up_acc, inner, forked_inner, share_ref, prev,
     kept, core_out, core_in, y_out, y_in, z_out, z_in,
     w_sem, g_send, g_recv, r_send, r_recv, p_sem) = scratch
    rows, width = hidden_ref.shape
    hidden_units = gate_w.shape[1]
    total = rows * experts
    half = total // 2
    quarter = total // 4
    gw = width // gc
    rw = width // rc
    bits = zs.bit_length() - 1

    w_copies = [
        pltpu.make_async_copy(gate_hbm.at[0], gate_w, w_sem.at[0]),
        pltpu.make_async_copy(up_hbm.at[0], up_w, w_sem.at[1]),
        pltpu.make_async_copy(down_hbm.at[0], down_w, w_sem.at[2]),
    ]
    for copy in w_copies:
        copy.start()

    me = lax.axis_index("expert")
    core = lax.rem(me, 2)
    y = lax.rem(lax.div(me, 2), 2)
    z_bits = [lax.rem(lax.div(me, 4 << b), 2) for b in range(bits)]

    def flipped(dz, dy, dc):
        index = (1 - core if dc else core) + 2 * (1 - y if dy else y)
        for b in range(bits):
            index = index + (4 << b) * (1 - z_bits[b] if (dz >> b) & 1 else z_bits[b])
        return index

    z_peers = [flipped(dz, 0, 0) for dz in range(zs)]
    y_peer = flipped(0, 1, 0)
    core_peer = flipped(0, 0, 1)
    after = lax.rem(me + 1, experts)
    before = lax.rem(me + experts - 1, experts)

    barrier = pltpu.get_barrier_semaphore()
    greeted = z_peers[1:] + [y_peer, core_peer, after, before]
    for peer in greeted:
        pl.semaphore_signal(barrier, inc=1, device_id={"expert": peer}, device_id_type=MESH)

    own = hidden_ref[...].astype(jnp.float32)
    scale = lax.rsqrt(jnp.mean(own * own, axis=-1, keepdims=True) + 1e-06)
    normed = (own * scale * gain_ref[...]).astype(jnp.bfloat16)
    row_no = lax.broadcasted_iota(jnp.int32, (rows, LANES), 0)
    lane = lax.broadcasted_iota(jnp.int32, (rows, LANES), 1)
    parents = jnp.zeros((rows, LANES), jnp.int32)
    for r in range(rows):
        parents = jnp.where(row_no == r, parent_ref[r], parents)
    share = weight_ref[...] / jnp.sum(weight_ref[...], axis=-1, keepdims=True)
    ids = ids_ref[...]
    spread = jnp.zeros((rows, LANES), jnp.float32)
    lane_expert = lax.rem(lane, experts)
    for k in range(ids.shape[1]):
        spread = spread + jnp.where(lane_expert == ids[:, k:k + 1], share[:, k:k + 1], 0.0)
    high = spread.astype(jnp.bfloat16).astype(jnp.float32)
    middle = (spread - high).astype(jnp.bfloat16).astype(jnp.float32)
    low = spread - high - middle
    meta = jnp.where(
        lane < experts, high,
        jnp.where(lane < 2 * experts, middle,
                  jnp.where(lane < 3 * experts, low,
                            jnp.where(lane == 3 * experts, parents.astype(jnp.float32), 0.0))))
    for k in range(gc):
        rows_in[k][0:rows, 0:gw] = normed[:, k * gw:(k + 1) * gw]
    rows_in[0][0:rows, gw:gw + LANES] = meta.astype(jnp.bfloat16)

    pl.semaphore_wait(barrier, len(greeted))

    sends = []

    def remote(src, dst, send, recv, peer):
        return pltpu.make_async_remote_copy(
            src_ref=src, dst_ref=dst, send_sem=send, recv_sem=recv,
            device_id={"expert": peer}, device_id_type=MESH)

    def gather(k, first, count, target, number, peer):
        buf = rows_in[k]
        return remote(buf.at[pl.ds(first * rows, count * rows), :],
                      buf.at[pl.ds(target * rows, count * rows), :],
                      g_send.at[k, number], g_recv.at[k, number], peer)

    def go(copy):
        copy.start()
        sends.append(copy)
        return copy

    z_copies, y_copies, c_copies = [], [], []
    for k in range(gc):
        z_copies.append([go(gather(k, 0, 1, dz, dz - 1, z_peers[dz])) for dz in range(1, zs)])
        y_copies.append([go(gather(k, 0, 1, zs, zs, y_peer))])
        c_copies.append([go(gather(k, 0, 1, 2 * zs, zs + 1, core_peer))])
    before_copy = None
    tile = 256
    for step in range(gc + 2):
        k = step
        if k < gc:
            for copy in z_copies[k]:
                copy.wait_recv()
            y_copies[k].append(go(gather(k, 1, zs - 1, zs + 1, zs + 2, y_peer)))
            c_copies[k].append(go(gather(k, 1, zs - 1, 2 * zs + 1, zs + 3, core_peer)))
        k = step - 1
        if 0 <= k < gc:
            for copy in y_copies[k]:
                copy.wait_recv()
            c_copies[k].append(go(gather(k, zs, zs, 3 * zs, zs + 4, core_peer)))
        k = step - 2
        if 0 <= k < gc:
            for copy in c_copies[k]:
                copy.wait_recv()
            if k == 0:
                w_copies[0].wait()
                w_copies[1].wait()
            if k == gc - 1:
                before_copy = go(remote(hidden_ref, prev, p_sem.at[0], p_sem.at[1], after))

            @pl.loop(0, hidden_units // tile)
            def _(t):
                columns = pl.ds(pl.multiple_of(t * tile, tile), tile)
                block = rows_in[k][:, 0:gw]
                gate = jnp.dot(block, gate_w[k * gw:(k + 1) * gw, columns],
                               preferred_element_type=jnp.float32)
                up = jnp.dot(block, up_w[k * gw:(k + 1) * gw, columns],
                             preferred_element_type=jnp.float32)
                if k > 0:
                    gate = gate + gate_acc[:, columns]
                    up = up + up_acc[:, columns]
                if k < gc - 1:
                    gate_acc[:, columns] = gate
                    up_acc[:, columns] = up
                else:
                    inner[:, columns] = (gate / (1.0 + jnp.exp(-gate)) * up).astype(jnp.bfloat16)

            if k == 0:
                facts = rows_in[0][:, gw:gw + LANES].astype(jnp.float32)
                lanes = lax.broadcasted_iota(jnp.int32, (total, LANES), 1)
                mine = (lax.rem(lanes, experts) == me) & (lanes < 3 * experts)
                share_ref[...] = jnp.sum(jnp.where(mine, facts, 0.0), axis=1, keepdims=True)
                wanted = facts[:, 3 * experts:3 * experts + 1]
                held = lax.broadcasted_iota(jnp.int32, (total, total), 1)
                slot = lax.div(held, rows)
                dz = lax.rem(slot, zs)
                dy = lax.rem(lax.div(slot, zs), 2)
                dc = lax.div(slot, 2 * zs)
                owner = dc + core - 2 * core * dc + 2 * (dy + y - 2 * y * dy)
                for b in range(bits):
                    bit = lax.rem(lax.div(dz, 1 << b), 2)
                    owner = owner + (4 << b) * (bit + z_bits[b] - 2 * z_bits[b] * bit)
                at = (owner * rows + lax.rem(held, rows)).astype(jnp.float32)
                choose = jnp.where(at == wanted, 1.0, 0.0).astype(jnp.bfloat16)

    forked_inner[...] = jnp.dot(
        choose, inner[...], preferred_element_type=jnp.float32).astype(jnp.bfloat16)
    w_copies[2].wait()
    core_copies = []
    for k in range(rc):

        @pl.loop(0, rw // tile)
        def _(t):
            columns = pl.ds(pl.multiple_of(k * rw + t * tile, tile), tile)
            local = pl.ds(pl.multiple_of(t * tile, tile), tile)
            result = jnp.dot(forked_inner[...], down_w[:, columns],
                             preferred_element_type=jnp.float32)
            result = result.astype(jnp.bfloat16).astype(jnp.float32) * share_ref[...]
            kept[k, :, local] = result[0:half]
            core_out[k, :, local] = result[half:total].astype(jnp.bfloat16)

        core_copies.append(go(remote(core_out.at[k], core_in.at[k],
                                     r_send.at[k, 0], r_recv.at[k, 0], core_peer)))

    y_back = []
    for k in range(rc):
        core_copies[k].wait_recv()
        y_out[k] = (kept[k, quarter:half] + core_in[k, quarter:half].astype(jnp.float32)
                    ).astype(jnp.bfloat16)
        y_back.append(go(remote(y_out.at[k], y_in.at[k],
                                r_send.at[k, 1], r_recv.at[k, 1], y_peer)))

    before_copy.wait_recv()
    pool_no = lax.broadcasted_iota(jnp.int32, (rows, 2 * rows), 1)
    pick = jnp.where(parents[:, 0:2 * rows] - (me - 1) * rows == pool_no, 1.0, 0.0)
    pick = pick.astype(jnp.bfloat16)

    z_back = []
    for k in range(rc):
        y_back[k].wait_recv()
        summed = (kept[k, 0:quarter] + core_in[k, 0:quarter].astype(jnp.float32)
                  + y_in[k].astype(jnp.float32))
        kept[k, 0:rows] = summed[0:rows]
        z_out[k] = summed[rows:quarter].astype(jnp.bfloat16)
        z_back.append([
            go(remote(z_out.at[k, pl.ds((dz - 1) * rows, rows), :],
                      z_in.at[k, pl.ds((dz - 1) * rows, rows), :],
                      r_send.at[k, 1 + dz], r_recv.at[k, 1 + dz], z_peers[dz]))
            for dz in range(1, zs)])

    for k in range(rc):
        columns = slice(k * rw, (k + 1) * rw)
        forked = (
            jnp.dot(pick[:, 0:rows], prev[:, columns], preferred_element_type=jnp.float32)
            + jnp.dot(pick[:, rows:2 * rows], hidden_ref[:, columns],
                      preferred_element_type=jnp.float32))
        mixed = kept[k, 0:rows]
        for dz in range(1, zs):
            z_back[k][dz - 1].wait_recv()
            mixed = mixed + z_in[k, (dz - 1) * rows:dz * rows].astype(jnp.float32)
        out_ref[:, columns] = (forked + mixed).astype(out_ref.dtype)

    for copy in sends:
        copy.wait_send()


def dense(hidden, parent, expert_ids, route_weight, norm_gain, w_gate, w_up, w_down):
    rows, width = hidden.shape
    experts = lax.axis_size("expert")
    zs = experts // 4
    units = w_gate.shape[2]
    total = rows * experts
    gc, rc = GATHER_CHUNKS, RETURN_CHUNKS
    gw, rw = width // gc, width // rc
    bf16, f32 = jnp.bfloat16, jnp.float32
    vmem = pl.BlockSpec(memory_space=pltpu.VMEM)
    hbm = pl.BlockSpec(memory_space=pl.ANY)
    return pl.pallas_call(
        functools.partial(dense_kernel, experts=experts, zs=zs),
        out_shape=jax.ShapeDtypeStruct((rows, width), hidden.dtype),
        in_specs=[pl.BlockSpec(memory_space=pltpu.SMEM), vmem, vmem, vmem, vmem, hbm, hbm, hbm],
        out_specs=vmem,
        scratch_shapes=[
            pltpu.VMEM((total, gw + (LANES if k == 0 else 0)), bf16) for k in range(gc)
        ] + [
            pltpu.VMEM((width, units), bf16),
            pltpu.VMEM((width, units), bf16),
            pltpu.VMEM((units, width), bf16),
            pltpu.VMEM((total, units), f32),
            pltpu.VMEM((total, units), f32),
            pltpu.VMEM((total, units), bf16),
            pltpu.VMEM((total, units), bf16),
            pltpu.VMEM((total, 1), f32),
            pltpu.VMEM((rows, width), bf16),
            pltpu.VMEM((rc, total // 2, rw), f32),
            pltpu.VMEM((rc, total // 2, rw), bf16),
            pltpu.VMEM((rc, total // 2, rw), bf16),
            pltpu.VMEM((rc, total // 4, rw), bf16),
            pltpu.VMEM((rc, total // 4, rw), bf16),
            pltpu.VMEM((rc, total // 4 - rows, rw), bf16),
            pltpu.VMEM((rc, total // 4 - rows, rw), bf16),
            pltpu.SemaphoreType.DMA((3,)),
            pltpu.SemaphoreType.DMA((gc, zs + 5)),
            pltpu.SemaphoreType.DMA((gc, zs + 5)),
            pltpu.SemaphoreType.DMA((rc, zs + 1)),
            pltpu.SemaphoreType.DMA((rc, zs + 1)),
            pltpu.SemaphoreType.DMA((2,)),
        ],
        compiler_params=pltpu.CompilerParams(
            collective_id=0, has_side_effects=True, vmem_limit_bytes=48 * 1024 * 1024),
    )(parent, hidden, expert_ids, route_weight, norm_gain.reshape(1, width),
      w_gate, w_up, w_down)


def shifted(shard, axis, by):
    peers = lax.axis_size(axis)
    pairs = [(i, i + by) for i in range(peers) if 0 <= i + by < peers]
    return lax.ppermute(shard, axis, pairs)


def routed(hidden, parent, expert_ids, route_weight, norm_gain, w_gate, w_up, w_down):
    row_count = hidden.shape[0]
    width = hidden.shape[1]
    route_count = expert_ids.shape[1]
    expert_count = lax.axis_size("expert")
    capacity = 2 * row_count * route_count // expert_count
    my_index = lax.axis_index("expert")
    first_row = my_index * row_count
    before = shifted(hidden, "expert", 1)
    pool = jnp.concatenate([before, hidden], axis=0)
    local_parent = parent - (first_row - row_count)
    forked = jnp.take(pool, local_parent, axis=0)
    forked_f = forked.astype(jnp.float32)
    scale_row = lax.rsqrt(jnp.mean(forked_f * forked_f, axis=-1, keepdims=True) + 1e-06)
    normed = (forked_f * scale_row * norm_gain).astype(jnp.bfloat16)
    share = route_weight / jnp.sum(route_weight, axis=-1, keepdims=True)
    flat_ids = expert_ids.reshape(-1)
    expert_range = jnp.arange(expert_count, dtype=jnp.int32)
    onehot = (flat_ids[:, None] == expert_range[None, :]).astype(jnp.int32)
    earlier = jnp.cumsum(onehot, axis=0) - onehot
    slot_no = jnp.sum(earlier * onehot, axis=1)
    target = flat_ids * capacity + slot_no
    slot_range = jnp.arange(expert_count * capacity, dtype=jnp.int32)
    placing = (target[None, :] == slot_range[:, None]).astype(jnp.bfloat16)
    repeated = jnp.repeat(normed, route_count, axis=0)
    outgoing = jnp.dot(placing, repeated, preferred_element_type=jnp.float32).astype(jnp.bfloat16)
    outgoing = outgoing.reshape(expert_count, capacity, width)
    block = lax.all_to_all(outgoing, "expert", split_axis=0, concat_axis=0, tiled=True)
    sources = block.shape[0]
    items = block.shape[1]
    inputs = block.reshape(sources * items, width)
    gate_val = jnp.dot(inputs, w_gate[0], preferred_element_type=jnp.float32)
    up_val = jnp.dot(inputs, w_up[0], preferred_element_type=jnp.float32)
    inner = (jax.nn.silu(gate_val) * up_val).astype(jnp.bfloat16)
    result = jnp.dot(inner, w_down[0], preferred_element_type=jnp.float32).astype(jnp.bfloat16)
    result = result.reshape(sources, items, width)
    returned = lax.all_to_all(result, "expert", split_axis=0, concat_axis=0, tiled=True)
    back_flat = returned.reshape(expert_count * capacity, width).astype(jnp.float32)
    target_rows = target.reshape(row_count, route_count)
    combining = jnp.sum(
        (target_rows[:, :, None] == slot_range[None, None, :]).astype(jnp.float32)
        * share[:, :, None],
        axis=1,
    )
    mixed = jnp.dot(
        combining, back_flat, precision=lax.Precision.HIGHEST, preferred_element_type=jnp.float32
    )
    return (forked_f + mixed).astype(jnp.bfloat16)


def per_device(hidden, *others):
    experts = lax.axis_size("expert")
    slots = 2 * hidden.shape[0] * others[1].shape[1]
    fits = hidden.shape[0] * experts <= min(slots, 256) and 3 * experts < LANES
    if fits and experts >= 8 and experts & (experts - 1) == 0:
        return dense(hidden, *others)
    return routed(hidden, *others)


def solution(mesh):
    in_specs = (
        P(("parts", "expert"), None),
        P(("parts", "expert")),
        P(("parts", "expert"), None),
        P(("parts", "expert"), None),
        P(),
        P("expert", None, None),
        P("expert", None, None),
        P("expert", None, None),
    )
    out_specs = P(("parts", "expert"), None)
    return jax.shard_map(
        per_device, mesh=mesh, in_specs=in_specs, out_specs=out_specs, check_vma=False
    )
```

```python
import functools

import jax
import jax.numpy as jnp
from jax import lax
from jax.experimental import pallas as pl
from jax.experimental.pallas import tpu as pltpu
from jax.sharding import PartitionSpec as P

MESH = pl.DeviceIdType.MESH
GATHER_CHUNKS = 1
RETURN_CHUNKS = 2
LANES = 128


def gather_order(chunks, zs):
    order, left = [], []
    for k in range(chunks):
        for dz in range(1, zs):
            order.append(("z", k, dz))
            if left:
                order.append(left.pop(0))
        order += left
        left = [("y", k, dz) for dz in range(zs)] + [("c", k, 0)]
    return order + left


def dense_kernel(
    parent_ref, hidden_hbm, ids_hbm, weight_hbm, gain_hbm, gate_hbm, up_hbm, down_hbm,
    out_ref,
    *scratch,
    experts, zs,
):
    gc, rc = GATHER_CHUNKS, RETURN_CHUNKS
    scratch = list(scratch)
    rows_in = [scratch.pop(0) for _ in range(gc)]
    (gate_w, up_w, down_w, gate_acc, up_acc, inner, forked_inner, share_ref, prev,
     kept, core_out, core_in, y_out, y_in, z_out, z_in,
     hidden_ref, ids_ref, weight_ref, gain_ref,
     w_sem, g_send, g_recv, r_send, r_recv, p_sem) = scratch
    rows, width = hidden_ref.shape
    hidden_units = gate_w.shape[1]
    total = rows * experts
    half = total // 2
    quarter = total // 4
    gw = width // gc
    rw = width // rc
    bits = zs.bit_length() - 1
    row_bits = rows.bit_length() - 1

    w_copies = [
        pltpu.make_async_copy(gate_hbm.at[0], gate_w, w_sem.at[0]),
        pltpu.make_async_copy(up_hbm.at[0], up_w, w_sem.at[1]),
        pltpu.make_async_copy(down_hbm.at[0], down_w, w_sem.at[2]),
    ]
    small_copies = [
        pltpu.make_async_copy(hidden_hbm, hidden_ref, w_sem.at[3]),
        pltpu.make_async_copy(ids_hbm, ids_ref, w_sem.at[4]),
        pltpu.make_async_copy(weight_hbm, weight_ref, w_sem.at[5]),
        pltpu.make_async_copy(gain_hbm, gain_ref, w_sem.at[6]),
    ]
    for copy in small_copies + w_copies:
        copy.start()

    me = lax.axis_index("expert")
    core = lax.rem(me, 2)
    y = lax.rem(lax.div(me, 2), 2)
    z_bits = [lax.rem(lax.div(me, 4 << b), 2) for b in range(bits)]

    def flipped(dz, dy, dc):
        index = (1 - core if dc else core) + 2 * (1 - y if dy else y)
        for b in range(bits):
            index = index + (4 << b) * (1 - z_bits[b] if (dz >> b) & 1 else z_bits[b])
        return index

    z_peers = [flipped(dz, 0, 0) for dz in range(zs)]
    y_peer = flipped(0, 1, 0)
    core_peer = flipped(0, 0, 1)
    after = lax.rem(me + 1, experts)
    before = lax.rem(me + experts - 1, experts)

    barrier = pltpu.get_barrier_semaphore()
    greeted = z_peers[1:] + [y_peer, core_peer, after, before]
    for peer in greeted:
        pl.semaphore_signal(barrier, inc=1, device_id={"expert": peer}, device_id_type=MESH)

    for copy in small_copies:
        copy.wait()

    own = hidden_ref[...].astype(jnp.float32)
    scale = lax.rsqrt(jnp.mean(own * own, axis=-1, keepdims=True) + 1e-06)
    normed = (own * scale * gain_ref[...]).astype(jnp.bfloat16)
    row_no = lax.broadcasted_iota(jnp.int32, (rows, LANES), 0)
    lane = lax.broadcasted_iota(jnp.int32, (rows, LANES), 1)
    parents = jnp.zeros((rows, LANES), jnp.int32)
    for r in range(rows):
        parents = jnp.where(row_no == r, parent_ref[r], parents)
    weights = weight_ref[...].T
    share = weights / jnp.sum(weights, axis=-1, keepdims=True)
    ids = ids_ref[...].T
    spread = jnp.zeros((rows, LANES), jnp.float32)
    lane_expert = lane & (experts - 1)
    for k in range(ids.shape[1]):
        spread = spread + jnp.where(lane_expert == ids[:, k:k + 1], share[:, k:k + 1], 0.0)
    high = spread.astype(jnp.bfloat16).astype(jnp.float32)
    middle = (spread - high).astype(jnp.bfloat16).astype(jnp.float32)
    low = spread - high - middle
    meta = jnp.where(
        lane < experts, high,
        jnp.where(lane < 2 * experts, middle,
                  jnp.where(lane < 3 * experts, low,
                            jnp.where(lane == 3 * experts, parents.astype(jnp.float32), 0.0))))
    for k in range(gc):
        rows_in[k][0:rows, 0:gw] = normed[:, k * gw:(k + 1) * gw]
    rows_in[0][0:rows, gw:gw + LANES] = meta.astype(jnp.bfloat16)

    pl.semaphore_wait(barrier, len(greeted))

    sends = []

    def remote(src, dst, send, recv, peer):
        return pltpu.make_async_remote_copy(
            src_ref=src, dst_ref=dst, send_sem=send, recv_sem=recv,
            device_id={"expert": peer}, device_id_type=MESH)

    def gather(k, source, target, peer):
        buf = rows_in[k]
        return remote(buf.at[pl.ds(source * rows, rows), :], buf.at[pl.ds(target * rows, rows), :],
                      g_send.at[k, target], g_recv.at[k, target], peer)

    def go(copy):
        copy.start()
        sends.append(copy)
        return copy

    z_copies, y_copies, c_copies = [], [], []
    for k in range(gc):
        z_copies.append([None] + [go(gather(k, 0, dz, z_peers[dz])) for dz in range(1, zs)])
        y_copies.append([go(gather(k, 0, zs, y_peer))])
        c_copies.append([go(gather(k, 0, 2 * zs, core_peer))])
    before_copy = None
    tile = 256
    for stage, k, dz in gather_order(gc, zs):
        if stage == "z":
            z_copies[k][dz].wait_recv()
            y_copies[k].append(go(gather(k, dz, zs + dz, y_peer)))
            c_copies[k].append(go(gather(k, dz, 2 * zs + dz, core_peer)))
        elif stage == "y":
            y_copies[k][dz].wait_recv()
            c_copies[k].append(go(gather(k, zs + dz, 3 * zs + dz, core_peer)))
        else:
            for copy in c_copies[k]:
                copy.wait_recv()
            if k == 0:
                w_copies[0].wait()
                w_copies[1].wait()
            if k == gc - 1:
                before_copy = go(remote(hidden_ref, prev, p_sem.at[0], p_sem.at[1], after))

            @pl.loop(0, hidden_units // tile)
            def _(t):
                columns = pl.ds(pl.multiple_of(t * tile, tile), tile)
                block = rows_in[k][:, 0:gw]
                gate = jnp.dot(block, gate_w[k * gw:(k + 1) * gw, columns],
                               preferred_element_type=jnp.float32)
                up = jnp.dot(block, up_w[k * gw:(k + 1) * gw, columns],
                             preferred_element_type=jnp.float32)
                if k > 0:
                    gate = gate + gate_acc[:, columns]
                    up = up + up_acc[:, columns]
                if k < gc - 1:
                    gate_acc[:, columns] = gate
                    up_acc[:, columns] = up
                else:
                    inner[:, columns] = (gate / (1.0 + jnp.exp(-gate)) * up).astype(jnp.bfloat16)

            if k == 0:
                facts = rows_in[0][:, gw:gw + LANES].astype(jnp.float32)
                lanes = lax.broadcasted_iota(jnp.int32, (total, LANES), 1)
                mine = ((lanes & (experts - 1)) == me) & (lanes < 3 * experts)
                share_ref[...] = jnp.sum(jnp.where(mine, facts, 0.0), axis=1, keepdims=True)
                wanted = facts[:, 3 * experts:3 * experts + 1]
                held = lax.broadcasted_iota(jnp.int32, (8, total), 1)
                slot = held >> row_bits
                dz = slot & (zs - 1)
                dy = (slot >> bits) & 1
                dc = slot >> (bits + 1)
                owner = dc + core - 2 * core * dc + 2 * (dy + y - 2 * y * dy)
                for b in range(bits):
                    bit = (dz >> b) & 1
                    owner = owner + (4 << b) * (bit + z_bits[b] - 2 * z_bits[b] * bit)
                at = ((owner << row_bits) + (held & (rows - 1))).astype(jnp.float32)[0:1]
                choose = jnp.where(at == wanted, 1.0, 0.0).astype(jnp.bfloat16)

    forked_inner[...] = jnp.dot(
        choose, inner[...], preferred_element_type=jnp.float32).astype(jnp.bfloat16)
    w_copies[2].wait()
    core_copies = []
    for k in range(rc):

        @pl.loop(0, rw // tile)
        def _(t):
            columns = pl.ds(pl.multiple_of(k * rw + t * tile, tile), tile)
            local = pl.ds(pl.multiple_of(t * tile, tile), tile)
            result = jnp.dot(forked_inner[...], down_w[:, columns],
                             preferred_element_type=jnp.float32)
            result = result.astype(jnp.bfloat16).astype(jnp.float32) * share_ref[...]
            kept[k, :, local] = result[0:half]
            core_out[k, :, local] = result[half:total].astype(jnp.bfloat16)

        core_copies.append(go(remote(core_out.at[k], core_in.at[k],
                                     r_send.at[k, 0], r_recv.at[k, 0], core_peer)))

    y_back = []
    for k in range(rc):
        core_copies[k].wait_recv()
        y_back.append([None] * zs)
        for dz in reversed(range(zs)):
            here = pl.ds(dz * rows, rows)
            there = slice(quarter + dz * rows, quarter + (dz + 1) * rows)
            y_out[k, here] = (kept[k, there] + core_in[k, there].astype(jnp.float32)
                              ).astype(jnp.bfloat16)
            y_back[k][dz] = go(remote(y_out.at[k, here], y_in.at[k, here],
                                      r_send.at[k, 1 + dz], r_recv.at[k, 1 + dz], y_peer))

    before_copy.wait_recv()
    pool_no = lax.broadcasted_iota(jnp.int32, (rows, 2 * rows), 1)
    pick = jnp.where(parents[:, 0:2 * rows] - (me - 1) * rows == pool_no, 1.0, 0.0)
    pick = pick.astype(jnp.bfloat16)

    z_back = []
    for k in range(rc):
        z_back.append([None] * zs)
        for dz in reversed(range(zs)):
            y_back[k][dz].wait_recv()
            block = slice(dz * rows, (dz + 1) * rows)
            summed = (kept[k, block] + core_in[k, block].astype(jnp.float32)
                      + y_in[k, block].astype(jnp.float32))
            if dz == 0:
                kept[k, block] = summed
            else:
                place = pl.ds((dz - 1) * rows, rows)
                z_out[k, place] = summed.astype(jnp.bfloat16)
                z_back[k][dz] = go(remote(
                    z_out.at[k, place], z_in.at[k, place],
                    r_send.at[k, zs + dz], r_recv.at[k, zs + dz], z_peers[dz]))

    for k in range(rc):
        columns = slice(k * rw, (k + 1) * rw)
        forked = (
            jnp.dot(pick[:, 0:rows], prev[:, columns], preferred_element_type=jnp.float32)
            + jnp.dot(pick[:, rows:2 * rows], hidden_ref[:, columns],
                      preferred_element_type=jnp.float32))
        mixed = kept[k, 0:rows]
        for dz in range(1, zs):
            z_back[k][dz].wait_recv()
            mixed = mixed + z_in[k, (dz - 1) * rows:dz * rows].astype(jnp.float32)
        out_ref[:, columns] = (forked + mixed).astype(out_ref.dtype)

    for copy in sends:
        copy.wait_send()


def dense(hidden, parent, expert_ids, route_weight, norm_gain, w_gate, w_up, w_down):
    rows, width = hidden.shape
    experts = lax.axis_size("expert")
    zs = experts // 4
    units = w_gate.shape[2]
    top = expert_ids.shape[1]
    total = rows * experts
    gc, rc = GATHER_CHUNKS, RETURN_CHUNKS
    gw, rw = width // gc, width // rc
    bf16, f32 = jnp.bfloat16, jnp.float32
    vmem = pl.BlockSpec(memory_space=pltpu.VMEM)
    hbm = pl.BlockSpec(memory_space=pl.ANY)
    return pl.pallas_call(
        functools.partial(dense_kernel, experts=experts, zs=zs),
        out_shape=jax.ShapeDtypeStruct((rows, width), hidden.dtype),
        in_specs=[pl.BlockSpec(memory_space=pltpu.SMEM)] + [hbm] * 7,
        out_specs=vmem,
        scratch_shapes=[
            pltpu.VMEM((total, gw + (LANES if k == 0 else 0)), bf16) for k in range(gc)
        ] + [
            pltpu.VMEM((width, units), bf16),
            pltpu.VMEM((width, units), bf16),
            pltpu.VMEM((units, width), bf16),
            pltpu.VMEM((total, units), f32),
            pltpu.VMEM((total, units), f32),
            pltpu.VMEM((total, units), bf16),
            pltpu.VMEM((total, units), bf16),
            pltpu.VMEM((total, 1), f32),
            pltpu.VMEM((rows, width), bf16),
            pltpu.VMEM((rc, total // 2, rw), f32),
            pltpu.VMEM((rc, total // 2, rw), bf16),
            pltpu.VMEM((rc, total // 2, rw), bf16),
            pltpu.VMEM((rc, total // 4, rw), bf16),
            pltpu.VMEM((rc, total // 4, rw), bf16),
            pltpu.VMEM((rc, total // 4 - rows, rw), bf16),
            pltpu.VMEM((rc, total // 4 - rows, rw), bf16),
            pltpu.VMEM(hidden.shape, bf16),
            pltpu.VMEM((top, rows), jnp.int32),
            pltpu.VMEM((top, rows), f32),
            pltpu.VMEM((1, width), f32),
            pltpu.SemaphoreType.DMA((7,)),
            pltpu.SemaphoreType.DMA((gc, 4 * zs)),
            pltpu.SemaphoreType.DMA((gc, 4 * zs)),
            pltpu.SemaphoreType.DMA((rc, 2 * zs)),
            pltpu.SemaphoreType.DMA((rc, 2 * zs)),
            pltpu.SemaphoreType.DMA((2,)),
        ],
        compiler_params=pltpu.CompilerParams(
            collective_id=0, has_side_effects=True, vmem_limit_bytes=56 * 1024 * 1024),
    )(parent, hidden, expert_ids.T, route_weight.T, norm_gain.reshape(1, width),
      w_gate, w_up, w_down)


def shifted(shard, axis, by):
    peers = lax.axis_size(axis)
    pairs = [(i, i + by) for i in range(peers) if 0 <= i + by < peers]
    return lax.ppermute(shard, axis, pairs)


def routed(hidden, parent, expert_ids, route_weight, norm_gain, w_gate, w_up, w_down):
    row_count = hidden.shape[0]
    width = hidden.shape[1]
    route_count = expert_ids.shape[1]
    expert_count = lax.axis_size("expert")
    capacity = 2 * row_count * route_count // expert_count
    my_index = lax.axis_index("expert")
    first_row = my_index * row_count
    before = shifted(hidden, "expert", 1)
    pool = jnp.concatenate([before, hidden], axis=0)
    local_parent = parent - (first_row - row_count)
    forked = jnp.take(pool, local_parent, axis=0)
    forked_f = forked.astype(jnp.float32)
    scale_row = lax.rsqrt(jnp.mean(forked_f * forked_f, axis=-1, keepdims=True) + 1e-06)
    normed = (forked_f * scale_row * norm_gain).astype(jnp.bfloat16)
    share = route_weight / jnp.sum(route_weight, axis=-1, keepdims=True)
    flat_ids = expert_ids.reshape(-1)
    expert_range = jnp.arange(expert_count, dtype=jnp.int32)
    onehot = (flat_ids[:, None] == expert_range[None, :]).astype(jnp.int32)
    earlier = jnp.cumsum(onehot, axis=0) - onehot
    slot_no = jnp.sum(earlier * onehot, axis=1)
    target = flat_ids * capacity + slot_no
    slot_range = jnp.arange(expert_count * capacity, dtype=jnp.int32)
    placing = (target[None, :] == slot_range[:, None]).astype(jnp.bfloat16)
    repeated = jnp.repeat(normed, route_count, axis=0)
    outgoing = jnp.dot(placing, repeated, preferred_element_type=jnp.float32).astype(jnp.bfloat16)
    outgoing = outgoing.reshape(expert_count, capacity, width)
    block = lax.all_to_all(outgoing, "expert", split_axis=0, concat_axis=0, tiled=True)
    sources = block.shape[0]
    items = block.shape[1]
    inputs = block.reshape(sources * items, width)
    gate_val = jnp.dot(inputs, w_gate[0], preferred_element_type=jnp.float32)
    up_val = jnp.dot(inputs, w_up[0], preferred_element_type=jnp.float32)
    inner = (jax.nn.silu(gate_val) * up_val).astype(jnp.bfloat16)
    result = jnp.dot(inner, w_down[0], preferred_element_type=jnp.float32).astype(jnp.bfloat16)
    result = result.reshape(sources, items, width)
    returned = lax.all_to_all(result, "expert", split_axis=0, concat_axis=0, tiled=True)
    back_flat = returned.reshape(expert_count * capacity, width).astype(jnp.float32)
    target_rows = target.reshape(row_count, route_count)
    combining = jnp.sum(
        (target_rows[:, :, None] == slot_range[None, None, :]).astype(jnp.float32)
        * share[:, :, None],
        axis=1,
    )
    mixed = jnp.dot(
        combining, back_flat, precision=lax.Precision.HIGHEST, preferred_element_type=jnp.float32
    )
    return (forked_f + mixed).astype(jnp.bfloat16)


def per_device(hidden, *others):
    experts = lax.axis_size("expert")
    slots = 2 * hidden.shape[0] * others[1].shape[1]
    fits = hidden.shape[0] * experts <= min(slots, 256) and 3 * experts < LANES
    rows = hidden.shape[0]
    if fits and experts >= 8 and experts & (experts - 1) == 0 and rows & (rows - 1) == 0:
        return dense(hidden, *others)
    return routed(hidden, *others)


def solution(mesh):
    in_specs = (
        P(("parts", "expert"), None),
        P(("parts", "expert")),
        P(("parts", "expert"), None),
        P(("parts", "expert"), None),
        P(),
        P("expert", None, None),
        P("expert", None, None),
        P("expert", None, None),
    )
    out_specs = P(("parts", "expert"), None)
    return jax.shard_map(
        per_device, mesh=mesh, in_specs=in_specs, out_specs=out_specs, check_vma=False
    )
```

```python
import functools

import jax
import jax.numpy as jnp
from jax import lax
from jax.experimental import pallas as pl
from jax.experimental.pallas import tpu as pltpu
from jax.sharding import PartitionSpec as P

MESH = pl.DeviceIdType.MESH
GATHER_CHUNKS = 1
RETURN_CHUNKS = 2
LANES = 128


def gather_order(chunks, zs):
    order, left = [], []
    for k in range(chunks):
        for dz in range(1, zs):
            order.append(("z", k, dz))
            if left:
                order.append(left.pop(0))
        order += left
        left = [("y", k, dz) for dz in range(zs)] + [("c", k, 0)]
    return order + left


def dense_kernel(
    parent_ref, hidden_hbm, ids_hbm, weight_hbm, gain_hbm, gate_hbm, up_hbm, down_hbm,
    out_ref,
    *scratch,
    experts, zs,
):
    gc, rc = GATHER_CHUNKS, RETURN_CHUNKS
    scratch = list(scratch)
    rows_in = [scratch.pop(0) for _ in range(gc)]
    (gate_w, up_w, down_w, gate_acc, up_acc, inner, forked_inner, share_ref, prev,
     kept, core_out, core_in, y_out, y_in, z_out, z_in,
     hidden_ref, ids_ref, weight_ref, gain_ref,
     w_sem, g_send, g_recv, r_send, r_recv, p_sem) = scratch
    rows, width = hidden_ref.shape
    hidden_units = gate_w.shape[1]
    total = rows * experts
    half = total // 2
    quarter = total // 4
    gw = width // gc
    rw = width // rc
    bits = zs.bit_length() - 1
    row_bits = rows.bit_length() - 1

    w_copies = [
        pltpu.make_async_copy(gate_hbm.at[0], gate_w, w_sem.at[0]),
        pltpu.make_async_copy(up_hbm.at[0], up_w, w_sem.at[1]),
        pltpu.make_async_copy(down_hbm.at[0], down_w, w_sem.at[2]),
    ]
    small_copies = [
        pltpu.make_async_copy(hidden_hbm, hidden_ref, w_sem.at[3]),
        pltpu.make_async_copy(ids_hbm, ids_ref, w_sem.at[4]),
        pltpu.make_async_copy(weight_hbm, weight_ref, w_sem.at[5]),
        pltpu.make_async_copy(gain_hbm, gain_ref, w_sem.at[6]),
    ]
    for copy in small_copies + w_copies:
        copy.start()

    me = lax.axis_index("expert")
    core = lax.rem(me, 2)
    y = lax.rem(lax.div(me, 2), 2)
    z_bits = [lax.rem(lax.div(me, 4 << b), 2) for b in range(bits)]

    def flipped(dz, dy, dc):
        index = (1 - core if dc else core) + 2 * (1 - y if dy else y)
        for b in range(bits):
            index = index + (4 << b) * (1 - z_bits[b] if (dz >> b) & 1 else z_bits[b])
        return index

    z_peers = [flipped(dz, 0, 0) for dz in range(zs)]
    y_peer = flipped(0, 1, 0)
    core_peer = flipped(0, 0, 1)
    after = lax.rem(me + 1, experts)
    before = lax.rem(me + experts - 1, experts)

    barrier = pltpu.get_barrier_semaphore()
    greeted = z_peers[1:] + [y_peer, core_peer, after, before]
    for peer in greeted:
        pl.semaphore_signal(barrier, inc=1, device_id={"expert": peer}, device_id_type=MESH)

    for copy in small_copies:
        copy.wait()

    own = hidden_ref[...].astype(jnp.float32)
    scale = lax.rsqrt(jnp.mean(own * own, axis=-1, keepdims=True) + 1e-06)
    normed = (own * scale * gain_ref[...]).astype(jnp.bfloat16)
    row_no = lax.broadcasted_iota(jnp.int32, (rows, LANES), 0)
    lane = lax.broadcasted_iota(jnp.int32, (rows, LANES), 1)
    parents = jnp.zeros((rows, LANES), jnp.int32)
    for r in range(rows):
        parents = jnp.where(row_no == r, parent_ref[r], parents)
    weights = weight_ref[...].T
    share = weights / jnp.sum(weights, axis=-1, keepdims=True)
    ids = ids_ref[...].T
    spread = jnp.zeros((rows, LANES), jnp.float32)
    lane_expert = lane & (experts - 1)
    for k in range(ids.shape[1]):
        spread = spread + jnp.where(lane_expert == ids[:, k:k + 1], share[:, k:k + 1], 0.0)
    high = spread.astype(jnp.bfloat16).astype(jnp.float32)
    middle = (spread - high).astype(jnp.bfloat16).astype(jnp.float32)
    low = spread - high - middle
    meta = jnp.where(
        lane < experts, high,
        jnp.where(lane < 2 * experts, middle,
                  jnp.where(lane < 3 * experts, low,
                            jnp.where(lane == 3 * experts, parents.astype(jnp.float32), 0.0))))
    for k in range(gc):
        rows_in[k][0:rows, 0:gw] = normed[:, k * gw:(k + 1) * gw]
    rows_in[0][0:rows, gw:gw + LANES] = meta.astype(jnp.bfloat16)

    pl.semaphore_wait(barrier, len(greeted))

    sends = []

    def remote(src, dst, send, recv, peer):
        return pltpu.make_async_remote_copy(
            src_ref=src, dst_ref=dst, send_sem=send, recv_sem=recv,
            device_id={"expert": peer}, device_id_type=MESH)

    def gather(k, source, target, peer):
        buf = rows_in[k]
        return remote(buf.at[pl.ds(source * rows, rows), :], buf.at[pl.ds(target * rows, rows), :],
                      g_send.at[k, target], g_recv.at[k, target], peer)

    def go(copy):
        copy.start()
        sends.append(copy)
        return copy

    z_copies, y_copies, c_copies = [], [], []
    for k in range(gc):
        z_copies.append([None] + [go(gather(k, 0, dz, z_peers[dz])) for dz in range(1, zs)])
        y_copies.append([go(gather(k, 0, zs, y_peer))])
        c_copies.append([go(gather(k, 0, 2 * zs, core_peer))])
    before_copy = None
    tile = 256
    for stage, k, dz in gather_order(gc, zs):
        if stage == "z":
            z_copies[k][dz].wait_recv()
            y_copies[k].append(go(gather(k, dz, zs + dz, y_peer)))
            c_copies[k].append(go(gather(k, dz, 2 * zs + dz, core_peer)))
        elif stage == "y":
            y_copies[k][dz].wait_recv()
            c_copies[k].append(go(gather(k, zs + dz, 3 * zs + dz, core_peer)))
        else:
            for copy in c_copies[k]:
                copy.wait_recv()
            if k == 0:
                w_copies[0].wait()
                w_copies[1].wait()
            if k == gc - 1:
                before_copy = go(remote(hidden_ref, prev, p_sem.at[0], p_sem.at[1], after))

            @pl.loop(0, hidden_units // tile, unroll=True)
            def _(t):
                columns = pl.ds(pl.multiple_of(t * tile, tile), tile)
                block = rows_in[k][:, 0:gw]
                gate = jnp.dot(block, gate_w[k * gw:(k + 1) * gw, columns],
                               preferred_element_type=jnp.float32)
                up = jnp.dot(block, up_w[k * gw:(k + 1) * gw, columns],
                             preferred_element_type=jnp.float32)
                if k > 0:
                    gate = gate + gate_acc[:, columns]
                    up = up + up_acc[:, columns]
                if k < gc - 1:
                    gate_acc[:, columns] = gate
                    up_acc[:, columns] = up
                else:
                    inner[:, columns] = (gate / (1.0 + jnp.exp(-gate)) * up).astype(jnp.bfloat16)

            if k == 0:
                facts = rows_in[0][:, gw:gw + LANES].astype(jnp.float32)
                lanes = lax.broadcasted_iota(jnp.int32, (total, LANES), 1)
                mine = ((lanes & (experts - 1)) == me) & (lanes < 3 * experts)
                share_ref[...] = jnp.sum(jnp.where(mine, facts, 0.0), axis=1, keepdims=True)
                wanted = facts[:, 3 * experts:3 * experts + 1]
                held = lax.broadcasted_iota(jnp.int32, (8, total), 1)
                slot = held >> row_bits
                dz = slot & (zs - 1)
                dy = (slot >> bits) & 1
                dc = slot >> (bits + 1)
                owner = dc + core - 2 * core * dc + 2 * (dy + y - 2 * y * dy)
                for b in range(bits):
                    bit = (dz >> b) & 1
                    owner = owner + (4 << b) * (bit + z_bits[b] - 2 * z_bits[b] * bit)
                at = ((owner << row_bits) + (held & (rows - 1))).astype(jnp.float32)[0:1]
                choose = jnp.where(at == wanted, 1.0, 0.0).astype(jnp.bfloat16)

    forked_inner[...] = jnp.dot(
        choose, inner[...], preferred_element_type=jnp.float32).astype(jnp.bfloat16)
    w_copies[2].wait()
    core_copies = []
    for k in range(rc):

        @pl.loop(0, rw // tile, unroll=True)
        def _(t):
            columns = pl.ds(pl.multiple_of(k * rw + t * tile, tile), tile)
            local = pl.ds(pl.multiple_of(t * tile, tile), tile)
            result = jnp.dot(forked_inner[...], down_w[:, columns],
                             preferred_element_type=jnp.float32)
            result = result.astype(jnp.bfloat16).astype(jnp.float32) * share_ref[...]
            kept[k, :, local] = result[0:half]
            core_out[k, :, local] = result[half:total].astype(jnp.bfloat16)

        core_copies.append(go(remote(core_out.at[k], core_in.at[k],
                                     r_send.at[k, 0], r_recv.at[k, 0], core_peer)))

    y_back = []
    for k in range(rc):
        core_copies[k].wait_recv()
        y_back.append([None] * zs)
        for dz in reversed(range(zs)):
            here = pl.ds(dz * rows, rows)
            there = slice(quarter + dz * rows, quarter + (dz + 1) * rows)
            y_out[k, here] = (kept[k, there] + core_in[k, there].astype(jnp.float32)
                              ).astype(jnp.bfloat16)
            y_back[k][dz] = go(remote(y_out.at[k, here], y_in.at[k, here],
                                      r_send.at[k, 1 + dz], r_recv.at[k, 1 + dz], y_peer))

    before_copy.wait_recv()
    pool_no = lax.broadcasted_iota(jnp.int32, (rows, 2 * rows), 1)
    pick = jnp.where(parents[:, 0:2 * rows] - (me - 1) * rows == pool_no, 1.0, 0.0)
    pick = pick.astype(jnp.bfloat16)

    z_back = []
    for k in range(rc):
        z_back.append([None] * zs)
        for dz in reversed(range(zs)):
            y_back[k][dz].wait_recv()
            block = slice(dz * rows, (dz + 1) * rows)
            summed = (kept[k, block] + core_in[k, block].astype(jnp.float32)
                      + y_in[k, block].astype(jnp.float32))
            if dz == 0:
                kept[k, block] = summed
            else:
                place = pl.ds((dz - 1) * rows, rows)
                z_out[k, place] = summed.astype(jnp.bfloat16)
                z_back[k][dz] = go(remote(
                    z_out.at[k, place], z_in.at[k, place],
                    r_send.at[k, zs + dz], r_recv.at[k, zs + dz], z_peers[dz]))

    for k in range(rc):
        columns = slice(k * rw, (k + 1) * rw)
        forked = (
            jnp.dot(pick[:, 0:rows], prev[:, columns], preferred_element_type=jnp.float32)
            + jnp.dot(pick[:, rows:2 * rows], hidden_ref[:, columns],
                      preferred_element_type=jnp.float32))
        mixed = kept[k, 0:rows]
        for dz in range(1, zs):
            z_back[k][dz].wait_recv()
            mixed = mixed + z_in[k, (dz - 1) * rows:dz * rows].astype(jnp.float32)
        out_ref[:, columns] = (forked + mixed).astype(out_ref.dtype)

    for copy in sends:
        copy.wait_send()


def dense(hidden, parent, expert_ids, route_weight, norm_gain, w_gate, w_up, w_down):
    rows, width = hidden.shape
    experts = lax.axis_size("expert")
    zs = experts // 4
    units = w_gate.shape[2]
    top = expert_ids.shape[1]
    total = rows * experts
    gc, rc = GATHER_CHUNKS, RETURN_CHUNKS
    gw, rw = width // gc, width // rc
    bf16, f32 = jnp.bfloat16, jnp.float32
    vmem = pl.BlockSpec(memory_space=pltpu.VMEM)
    hbm = pl.BlockSpec(memory_space=pl.ANY)
    return pl.pallas_call(
        functools.partial(dense_kernel, experts=experts, zs=zs),
        out_shape=jax.ShapeDtypeStruct((rows, width), hidden.dtype),
        in_specs=[pl.BlockSpec(memory_space=pltpu.SMEM)] + [hbm] * 7,
        out_specs=vmem,
        scratch_shapes=[
            pltpu.VMEM((total, gw + (LANES if k == 0 else 0)), bf16) for k in range(gc)
        ] + [
            pltpu.VMEM((width, units), bf16),
            pltpu.VMEM((width, units), bf16),
            pltpu.VMEM((units, width), bf16),
            pltpu.VMEM((total, units), f32),
            pltpu.VMEM((total, units), f32),
            pltpu.VMEM((total, units), bf16),
            pltpu.VMEM((total, units), bf16),
            pltpu.VMEM((total, 1), f32),
            pltpu.VMEM((rows, width), bf16),
            pltpu.VMEM((rc, total // 2, rw), f32),
            pltpu.VMEM((rc, total // 2, rw), bf16),
            pltpu.VMEM((rc, total // 2, rw), bf16),
            pltpu.VMEM((rc, total // 4, rw), bf16),
            pltpu.VMEM((rc, total // 4, rw), bf16),
            pltpu.VMEM((rc, total // 4 - rows, rw), bf16),
            pltpu.VMEM((rc, total // 4 - rows, rw), bf16),
            pltpu.VMEM(hidden.shape, bf16),
            pltpu.VMEM((top, rows), jnp.int32),
            pltpu.VMEM((top, rows), f32),
            pltpu.VMEM((1, width), f32),
            pltpu.SemaphoreType.DMA((7,)),
            pltpu.SemaphoreType.DMA((gc, 4 * zs)),
            pltpu.SemaphoreType.DMA((gc, 4 * zs)),
            pltpu.SemaphoreType.DMA((rc, 2 * zs)),
            pltpu.SemaphoreType.DMA((rc, 2 * zs)),
            pltpu.SemaphoreType.DMA((2,)),
        ],
        compiler_params=pltpu.CompilerParams(
            collective_id=0, has_side_effects=True, vmem_limit_bytes=56 * 1024 * 1024),
    )(parent, hidden, expert_ids.T, route_weight.T, norm_gain.reshape(1, width),
      w_gate, w_up, w_down)


def shifted(shard, axis, by):
    peers = lax.axis_size(axis)
    pairs = [(i, i + by) for i in range(peers) if 0 <= i + by < peers]
    return lax.ppermute(shard, axis, pairs)


def routed(hidden, parent, expert_ids, route_weight, norm_gain, w_gate, w_up, w_down):
    row_count = hidden.shape[0]
    width = hidden.shape[1]
    route_count = expert_ids.shape[1]
    expert_count = lax.axis_size("expert")
    capacity = 2 * row_count * route_count // expert_count
    my_index = lax.axis_index("expert")
    first_row = my_index * row_count
    before = shifted(hidden, "expert", 1)
    pool = jnp.concatenate([before, hidden], axis=0)
    local_parent = parent - (first_row - row_count)
    forked = jnp.take(pool, local_parent, axis=0)
    forked_f = forked.astype(jnp.float32)
    scale_row = lax.rsqrt(jnp.mean(forked_f * forked_f, axis=-1, keepdims=True) + 1e-06)
    normed = (forked_f * scale_row * norm_gain).astype(jnp.bfloat16)
    share = route_weight / jnp.sum(route_weight, axis=-1, keepdims=True)
    flat_ids = expert_ids.reshape(-1)
    expert_range = jnp.arange(expert_count, dtype=jnp.int32)
    onehot = (flat_ids[:, None] == expert_range[None, :]).astype(jnp.int32)
    earlier = jnp.cumsum(onehot, axis=0) - onehot
    slot_no = jnp.sum(earlier * onehot, axis=1)
    target = flat_ids * capacity + slot_no
    slot_range = jnp.arange(expert_count * capacity, dtype=jnp.int32)
    placing = (target[None, :] == slot_range[:, None]).astype(jnp.bfloat16)
    repeated = jnp.repeat(normed, route_count, axis=0)
    outgoing = jnp.dot(placing, repeated, preferred_element_type=jnp.float32).astype(jnp.bfloat16)
    outgoing = outgoing.reshape(expert_count, capacity, width)
    block = lax.all_to_all(outgoing, "expert", split_axis=0, concat_axis=0, tiled=True)
    sources = block.shape[0]
    items = block.shape[1]
    inputs = block.reshape(sources * items, width)
    gate_val = jnp.dot(inputs, w_gate[0], preferred_element_type=jnp.float32)
    up_val = jnp.dot(inputs, w_up[0], preferred_element_type=jnp.float32)
    inner = (jax.nn.silu(gate_val) * up_val).astype(jnp.bfloat16)
    result = jnp.dot(inner, w_down[0], preferred_element_type=jnp.float32).astype(jnp.bfloat16)
    result = result.reshape(sources, items, width)
    returned = lax.all_to_all(result, "expert", split_axis=0, concat_axis=0, tiled=True)
    back_flat = returned.reshape(expert_count * capacity, width).astype(jnp.float32)
    target_rows = target.reshape(row_count, route_count)
    combining = jnp.sum(
        (target_rows[:, :, None] == slot_range[None, None, :]).astype(jnp.float32)
        * share[:, :, None],
        axis=1,
    )
    mixed = jnp.dot(
        combining, back_flat, precision=lax.Precision.HIGHEST, preferred_element_type=jnp.float32
    )
    return (forked_f + mixed).astype(jnp.bfloat16)


def per_device(hidden, *others):
    experts = lax.axis_size("expert")
    slots = 2 * hidden.shape[0] * others[1].shape[1]
    fits = hidden.shape[0] * experts <= min(slots, 256) and 3 * experts < LANES
    rows = hidden.shape[0]
    if fits and experts >= 8 and experts & (experts - 1) == 0 and rows & (rows - 1) == 0:
        return dense(hidden, *others)
    return routed(hidden, *others)


def solution(mesh):
    in_specs = (
        P(("parts", "expert"), None),
        P(("parts", "expert")),
        P(("parts", "expert"), None),
        P(("parts", "expert"), None),
        P(),
        P("expert", None, None),
        P("expert", None, None),
        P("expert", None, None),
    )
    out_specs = P(("parts", "expert"), None)
    return jax.shard_map(
        per_device, mesh=mesh, in_specs=in_specs, out_specs=out_specs, check_vma=False
    )
```

```python
import functools

import jax
import jax.numpy as jnp
from jax import lax
from jax.experimental import pallas as pl
from jax.experimental.pallas import tpu as pltpu
from jax.sharding import PartitionSpec as P

MESH = pl.DeviceIdType.MESH
GATHER_CHUNKS = 1
RETURN_CHUNKS = 2
LANES = 128


def gather_order(chunks, zs):
    order, left = [], []
    for k in range(chunks):
        for dz in range(1, zs):
            order.append(("z", k, dz))
            if left:
                order.append(left.pop(0))
        order += left
        left = [("y", k, dz) for dz in range(zs)] + [("c", k, 0)]
    return order + left


def dense_kernel(
    parent_ref, hidden_hbm, ids_hbm, weight_hbm, gain_hbm, gate_hbm, up_hbm, down_hbm,
    out_ref,
    *scratch,
    experts, zs,
):
    gc, rc = GATHER_CHUNKS, RETURN_CHUNKS
    scratch = list(scratch)
    rows_in = [scratch.pop(0) for _ in range(gc)]
    (gate_w, up_w, down_w, gate_acc, up_acc, inner, forked_inner, share_ref, prev,
     kept, core_out, core_in, y_out, y_in, z_out, z_in,
     hidden_ref, ids_ref, weight_ref, gain_ref,
     w_sem, g_send, g_recv, r_send, r_recv, p_sem) = scratch
    rows, width = hidden_ref.shape
    hidden_units = gate_w.shape[1]
    total = rows * experts
    half = total // 2
    quarter = total // 4
    gw = width // gc
    rw = width // rc
    bits = zs.bit_length() - 1
    row_bits = rows.bit_length() - 1

    w_copies = [
        pltpu.make_async_copy(gate_hbm.at[0], gate_w, w_sem.at[0]),
        pltpu.make_async_copy(up_hbm.at[0], up_w, w_sem.at[1]),
        pltpu.make_async_copy(down_hbm.at[0], down_w, w_sem.at[2]),
    ]
    small_copies = [
        pltpu.make_async_copy(hidden_hbm, hidden_ref, w_sem.at[3]),
        pltpu.make_async_copy(ids_hbm, ids_ref, w_sem.at[4]),
        pltpu.make_async_copy(weight_hbm, weight_ref, w_sem.at[5]),
        pltpu.make_async_copy(gain_hbm, gain_ref, w_sem.at[6]),
    ]
    for copy in small_copies + w_copies:
        copy.start()

    me = lax.axis_index("expert")
    core = lax.rem(me, 2)
    y = lax.rem(lax.div(me, 2), 2)
    z_bits = [lax.rem(lax.div(me, 4 << b), 2) for b in range(bits)]

    def flipped(dz, dy, dc):
        index = (1 - core if dc else core) + 2 * (1 - y if dy else y)
        for b in range(bits):
            index = index + (4 << b) * (1 - z_bits[b] if (dz >> b) & 1 else z_bits[b])
        return index

    z_peers = [flipped(dz, 0, 0) for dz in range(zs)]
    y_peer = flipped(0, 1, 0)
    core_peer = flipped(0, 0, 1)
    after = lax.rem(me + 1, experts)
    before = lax.rem(me + experts - 1, experts)

    barrier = pltpu.get_barrier_semaphore()
    greeted = z_peers[1:] + [y_peer, core_peer, after, before]
    for peer in greeted:
        pl.semaphore_signal(barrier, inc=1, device_id={"expert": peer}, device_id_type=MESH)

    for copy in small_copies:
        copy.wait()

    own = hidden_ref[...].astype(jnp.float32)
    scale = lax.rsqrt(jnp.mean(own * own, axis=-1, keepdims=True) + 1e-06)
    normed = (own * scale * gain_ref[...]).astype(jnp.bfloat16)
    row_no = lax.broadcasted_iota(jnp.int32, (rows, LANES), 0)
    lane = lax.broadcasted_iota(jnp.int32, (rows, LANES), 1)
    parents = jnp.zeros((rows, LANES), jnp.int32)
    for r in range(rows):
        parents = jnp.where(row_no == r, parent_ref[r], parents)
    weights = weight_ref[...].T
    share = weights / jnp.sum(weights, axis=-1, keepdims=True)
    ids = ids_ref[...].T
    spread = jnp.zeros((rows, LANES), jnp.float32)
    lane_expert = lane & (experts - 1)
    for k in range(ids.shape[1]):
        spread = spread + jnp.where(lane_expert == ids[:, k:k + 1], share[:, k:k + 1], 0.0)
    high = spread.astype(jnp.bfloat16).astype(jnp.float32)
    middle = (spread - high).astype(jnp.bfloat16).astype(jnp.float32)
    low = spread - high - middle
    meta = jnp.where(
        lane < experts, high,
        jnp.where(lane < 2 * experts, middle,
                  jnp.where(lane < 3 * experts, low,
                            jnp.where(lane == 3 * experts, parents.astype(jnp.float32), 0.0))))
    for k in range(gc):
        rows_in[k][0:rows, 0:gw] = normed[:, k * gw:(k + 1) * gw]
    rows_in[0][0:rows, gw:gw + LANES] = meta.astype(jnp.bfloat16)

    pl.semaphore_wait(barrier, len(greeted))

    sends = []

    def remote(src, dst, send, recv, peer):
        return pltpu.make_async_remote_copy(
            src_ref=src, dst_ref=dst, send_sem=send, recv_sem=recv,
            device_id={"expert": peer}, device_id_type=MESH)

    def gather(k, source, target, peer):
        buf = rows_in[k]
        return remote(buf.at[pl.ds(source * rows, rows), :], buf.at[pl.ds(target * rows, rows), :],
                      g_send.at[k, target], g_recv.at[k, target], peer)

    def go(copy):
        copy.start()
        sends.append(copy)
        return copy

    z_copies, y_copies, c_copies = [], [], []
    for k in range(gc):
        z_copies.append([None] + [go(gather(k, 0, dz, z_peers[dz])) for dz in range(1, zs)])
        y_copies.append([go(gather(k, 0, zs, y_peer))])
        c_copies.append([go(gather(k, 0, 2 * zs, core_peer))])
    before_copy = None
    tile = 256
    for stage, k, dz in gather_order(gc, zs):
        if stage == "z":
            z_copies[k][dz].wait_recv()
            y_copies[k].append(go(gather(k, dz, zs + dz, y_peer)))
            c_copies[k].append(go(gather(k, dz, 2 * zs + dz, core_peer)))
        elif stage == "y":
            y_copies[k][dz].wait_recv()
            c_copies[k].append(go(gather(k, zs + dz, 3 * zs + dz, core_peer)))
        else:
            for copy in c_copies[k]:
                copy.wait_recv()
            if k == 0:
                w_copies[0].wait()
                w_copies[1].wait()
            if k == gc - 1:
                before_copy = go(remote(hidden_ref, prev, p_sem.at[0], p_sem.at[1], after))

            @pl.loop(0, hidden_units // tile, unroll=True)
            def _(t):
                columns = pl.ds(pl.multiple_of(t * tile, tile), tile)
                block = rows_in[k][:, 0:gw]
                gate = jnp.dot(block, gate_w[k * gw:(k + 1) * gw, columns],
                               preferred_element_type=jnp.float32)
                up = jnp.dot(block, up_w[k * gw:(k + 1) * gw, columns],
                             preferred_element_type=jnp.float32)
                if k > 0:
                    gate = gate + gate_acc[:, columns]
                    up = up + up_acc[:, columns]
                if k < gc - 1:
                    gate_acc[:, columns] = gate
                    up_acc[:, columns] = up
                else:
                    inner[:, columns] = (gate / (1.0 + jnp.exp(-gate)) * up).astype(jnp.bfloat16)

            if k == 0:
                facts = rows_in[0][:, gw:gw + LANES].astype(jnp.float32)
                lanes = lax.broadcasted_iota(jnp.int32, (total, LANES), 1)
                mine = ((lanes & (experts - 1)) == me) & (lanes < 3 * experts)
                share_ref[...] = jnp.sum(jnp.where(mine, facts, 0.0), axis=1, keepdims=True)
                wanted = facts[:, 3 * experts:3 * experts + 1]
                held = lax.broadcasted_iota(jnp.int32, (8, total), 1)
                slot = held >> row_bits
                dz = slot & (zs - 1)
                dy = (slot >> bits) & 1
                dc = slot >> (bits + 1)
                owner = dc + core - 2 * core * dc + 2 * (dy + y - 2 * y * dy)
                for b in range(bits):
                    bit = (dz >> b) & 1
                    owner = owner + (4 << b) * (bit + z_bits[b] - 2 * z_bits[b] * bit)
                at = ((owner << row_bits) + (held & (rows - 1))).astype(jnp.float32)[0:1]
                choose = jnp.where(at == wanted, 1.0, 0.0).astype(jnp.bfloat16)

    forked_inner[...] = jnp.dot(
        choose, inner[...], preferred_element_type=jnp.float32).astype(jnp.bfloat16)
    w_copies[2].wait()
    core_copies = []
    for k in range(rc):

        @pl.loop(0, rw // tile, unroll=True)
        def _(t):
            columns = pl.ds(pl.multiple_of(k * rw + t * tile, tile), tile)
            local = pl.ds(pl.multiple_of(t * tile, tile), tile)
            result = jnp.dot(forked_inner[...], down_w[:, columns],
                             preferred_element_type=jnp.float32)
            result = result.astype(jnp.bfloat16).astype(jnp.float32) * share_ref[...]
            kept[k, :, local] = result[0:half]
            core_out[k, :, local] = result[half:total].astype(jnp.bfloat16)

        core_copies.append([
            go(remote(core_out.at[k, pl.ds(first, quarter)], core_in.at[k, pl.ds(first, quarter)],
                      r_send.at[k, number], r_recv.at[k, number], core_peer))
            for first, number in ((quarter, 0), (0, 2 * zs))])

    y_back = []
    for k in range(rc):
        core_copies[k][0].wait_recv()
        y_back.append([None] * zs)
        for dz in reversed(range(zs)):
            here = pl.ds(dz * rows, rows)
            there = slice(quarter + dz * rows, quarter + (dz + 1) * rows)
            y_out[k, here] = (kept[k, there] + core_in[k, there].astype(jnp.float32)
                              ).astype(jnp.bfloat16)
            y_back[k][dz] = go(remote(y_out.at[k, here], y_in.at[k, here],
                                      r_send.at[k, 1 + dz], r_recv.at[k, 1 + dz], y_peer))

    before_copy.wait_recv()
    pool_no = lax.broadcasted_iota(jnp.int32, (rows, 2 * rows), 1)
    pick = jnp.where(parents[:, 0:2 * rows] - (me - 1) * rows == pool_no, 1.0, 0.0)
    pick = pick.astype(jnp.bfloat16)

    forked = []
    for k in range(rc):
        columns = slice(k * rw, (k + 1) * rw)
        forked.append(
            jnp.dot(pick[:, 0:rows], prev[:, columns], preferred_element_type=jnp.float32)
            + jnp.dot(pick[:, rows:2 * rows], hidden_ref[:, columns],
                      preferred_element_type=jnp.float32))

    z_back = []
    for k in range(rc):
        core_copies[k][1].wait_recv()
        z_back.append([None] * zs)
        for dz in reversed(range(zs)):
            y_back[k][dz].wait_recv()
            block = slice(dz * rows, (dz + 1) * rows)
            summed = (kept[k, block] + core_in[k, block].astype(jnp.float32)
                      + y_in[k, block].astype(jnp.float32))
            if dz == 0:
                kept[k, block] = summed
            else:
                place = pl.ds((dz - 1) * rows, rows)
                z_out[k, place] = summed.astype(jnp.bfloat16)
                z_back[k][dz] = go(remote(
                    z_out.at[k, place], z_in.at[k, place],
                    r_send.at[k, zs + dz], r_recv.at[k, zs + dz], z_peers[dz]))

    for k in range(rc):
        columns = slice(k * rw, (k + 1) * rw)
        mixed = kept[k, 0:rows]
        for dz in range(1, zs):
            z_back[k][dz].wait_recv()
            mixed = mixed + z_in[k, (dz - 1) * rows:dz * rows].astype(jnp.float32)
        out_ref[:, columns] = (forked[k] + mixed).astype(out_ref.dtype)

    for copy in sends:
        copy.wait_send()


def dense(hidden, parent, expert_ids, route_weight, norm_gain, w_gate, w_up, w_down):
    rows, width = hidden.shape
    experts = lax.axis_size("expert")
    zs = experts // 4
    units = w_gate.shape[2]
    top = expert_ids.shape[1]
    total = rows * experts
    gc, rc = GATHER_CHUNKS, RETURN_CHUNKS
    gw, rw = width // gc, width // rc
    bf16, f32 = jnp.bfloat16, jnp.float32
    vmem = pl.BlockSpec(memory_space=pltpu.VMEM)
    hbm = pl.BlockSpec(memory_space=pl.ANY)
    return pl.pallas_call(
        functools.partial(dense_kernel, experts=experts, zs=zs),
        out_shape=jax.ShapeDtypeStruct((rows, width), hidden.dtype),
        in_specs=[pl.BlockSpec(memory_space=pltpu.SMEM)] + [hbm] * 7,
        out_specs=vmem,
        scratch_shapes=[
            pltpu.VMEM((total, gw + (LANES if k == 0 else 0)), bf16) for k in range(gc)
        ] + [
            pltpu.VMEM((width, units), bf16),
            pltpu.VMEM((width, units), bf16),
            pltpu.VMEM((units, width), bf16),
            pltpu.VMEM((total, units), f32),
            pltpu.VMEM((total, units), f32),
            pltpu.VMEM((total, units), bf16),
            pltpu.VMEM((total, units), bf16),
            pltpu.VMEM((total, 1), f32),
            pltpu.VMEM((rows, width), bf16),
            pltpu.VMEM((rc, total // 2, rw), f32),
            pltpu.VMEM((rc, total // 2, rw), bf16),
            pltpu.VMEM((rc, total // 2, rw), bf16),
            pltpu.VMEM((rc, total // 4, rw), bf16),
            pltpu.VMEM((rc, total // 4, rw), bf16),
            pltpu.VMEM((rc, total // 4 - rows, rw), bf16),
            pltpu.VMEM((rc, total // 4 - rows, rw), bf16),
            pltpu.VMEM(hidden.shape, bf16),
            pltpu.VMEM((top, rows), jnp.int32),
            pltpu.VMEM((top, rows), f32),
            pltpu.VMEM((1, width), f32),
            pltpu.SemaphoreType.DMA((7,)),
            pltpu.SemaphoreType.DMA((gc, 4 * zs)),
            pltpu.SemaphoreType.DMA((gc, 4 * zs)),
            pltpu.SemaphoreType.DMA((rc, 2 * zs + 1)),
            pltpu.SemaphoreType.DMA((rc, 2 * zs + 1)),
            pltpu.SemaphoreType.DMA((2,)),
        ],
        compiler_params=pltpu.CompilerParams(
            collective_id=0, has_side_effects=True, vmem_limit_bytes=56 * 1024 * 1024),
    )(parent, hidden, expert_ids.T, route_weight.T, norm_gain.reshape(1, width),
      w_gate, w_up, w_down)


def shifted(shard, axis, by):
    peers = lax.axis_size(axis)
    pairs = [(i, i + by) for i in range(peers) if 0 <= i + by < peers]
    return lax.ppermute(shard, axis, pairs)


def routed(hidden, parent, expert_ids, route_weight, norm_gain, w_gate, w_up, w_down):
    row_count = hidden.shape[0]
    width = hidden.shape[1]
    route_count = expert_ids.shape[1]
    expert_count = lax.axis_size("expert")
    capacity = 2 * row_count * route_count // expert_count
    my_index = lax.axis_index("expert")
    first_row = my_index * row_count
    before = shifted(hidden, "expert", 1)
    pool = jnp.concatenate([before, hidden], axis=0)
    local_parent = parent - (first_row - row_count)
    forked = jnp.take(pool, local_parent, axis=0)
    forked_f = forked.astype(jnp.float32)
    scale_row = lax.rsqrt(jnp.mean(forked_f * forked_f, axis=-1, keepdims=True) + 1e-06)
    normed = (forked_f * scale_row * norm_gain).astype(jnp.bfloat16)
    share = route_weight / jnp.sum(route_weight, axis=-1, keepdims=True)
    flat_ids = expert_ids.reshape(-1)
    expert_range = jnp.arange(expert_count, dtype=jnp.int32)
    onehot = (flat_ids[:, None] == expert_range[None, :]).astype(jnp.int32)
    earlier = jnp.cumsum(onehot, axis=0) - onehot
    slot_no = jnp.sum(earlier * onehot, axis=1)
    target = flat_ids * capacity + slot_no
    slot_range = jnp.arange(expert_count * capacity, dtype=jnp.int32)
    placing = (target[None, :] == slot_range[:, None]).astype(jnp.bfloat16)
    repeated = jnp.repeat(normed, route_count, axis=0)
    outgoing = jnp.dot(placing, repeated, preferred_element_type=jnp.float32).astype(jnp.bfloat16)
    outgoing = outgoing.reshape(expert_count, capacity, width)
    block = lax.all_to_all(outgoing, "expert", split_axis=0, concat_axis=0, tiled=True)
    sources = block.shape[0]
    items = block.shape[1]
    inputs = block.reshape(sources * items, width)
    gate_val = jnp.dot(inputs, w_gate[0], preferred_element_type=jnp.float32)
    up_val = jnp.dot(inputs, w_up[0], preferred_element_type=jnp.float32)
    inner = (jax.nn.silu(gate_val) * up_val).astype(jnp.bfloat16)
    result = jnp.dot(inner, w_down[0], preferred_element_type=jnp.float32).astype(jnp.bfloat16)
    result = result.reshape(sources, items, width)
    returned = lax.all_to_all(result, "expert", split_axis=0, concat_axis=0, tiled=True)
    back_flat = returned.reshape(expert_count * capacity, width).astype(jnp.float32)
    target_rows = target.reshape(row_count, route_count)
    combining = jnp.sum(
        (target_rows[:, :, None] == slot_range[None, None, :]).astype(jnp.float32)
        * share[:, :, None],
        axis=1,
    )
    mixed = jnp.dot(
        combining, back_flat, precision=lax.Precision.HIGHEST, preferred_element_type=jnp.float32
    )
    return (forked_f + mixed).astype(jnp.bfloat16)


def per_device(hidden, *others):
    experts = lax.axis_size("expert")
    slots = 2 * hidden.shape[0] * others[1].shape[1]
    fits = hidden.shape[0] * experts <= min(slots, 256) and 3 * experts < LANES
    rows = hidden.shape[0]
    if fits and experts >= 8 and experts & (experts - 1) == 0 and rows & (rows - 1) == 0:
        return dense(hidden, *others)
    return routed(hidden, *others)


def solution(mesh):
    in_specs = (
        P(("parts", "expert"), None),
        P(("parts", "expert")),
        P(("parts", "expert"), None),
        P(("parts", "expert"), None),
        P(),
        P("expert", None, None),
        P("expert", None, None),
        P("expert", None, None),
    )
    out_specs = P(("parts", "expert"), None)
    return jax.shard_map(
        per_device, mesh=mesh, in_specs=in_specs, out_specs=out_specs, check_vma=False
    )
```

```python
import functools

import jax
import jax.numpy as jnp
from jax import lax
from jax.experimental import pallas as pl
from jax.experimental.pallas import tpu as pltpu
from jax.sharding import PartitionSpec as P

MESH = pl.DeviceIdType.MESH
GATHER_CHUNKS = 1
RETURN_CHUNKS = 2
LANES = 128


def gather_order(chunks, zs):
    order, left = [], []
    for k in range(chunks):
        for dz in range(1, zs):
            order.append(("z", k, dz))
            if left:
                order.append(left.pop(0))
        order += left
        left = [("y", k, dz) for dz in range(zs)] + [("c", k, 0)]
    return order + left


def dense_kernel(
    parent_ref, hidden_hbm, ids_hbm, weight_hbm, gain_hbm, gate_hbm, up_hbm, down_hbm,
    out_ref,
    *scratch,
    experts, zs,
):
    gc, rc = GATHER_CHUNKS, RETURN_CHUNKS
    scratch = list(scratch)
    rows_in = [scratch.pop(0) for _ in range(gc)]
    (gate_w, up_w, down_w, gate_acc, up_acc, inner, forked_inner, share_ref, prev,
     kept, core_out, core_in, y_out, y_in, z_out, z_in,
     hidden_ref, ids_ref, weight_ref, gain_ref,
     w_sem, g_send, g_recv, r_send, r_recv, p_sem) = scratch
    rows, width = hidden_ref.shape
    hidden_units = gate_w.shape[1]
    total = rows * experts
    half = total // 2
    quarter = total // 4
    gw = width // gc
    rw = width // rc
    bits = zs.bit_length() - 1
    row_bits = rows.bit_length() - 1

    me = lax.axis_index("expert")
    core = lax.rem(me, 2)
    y = lax.rem(lax.div(me, 2), 2)
    z_bits = [lax.rem(lax.div(me, 4 << b), 2) for b in range(bits)]

    def flipped(dz, dy, dc):
        index = (1 - core if dc else core) + 2 * (1 - y if dy else y)
        for b in range(bits):
            index = index + (4 << b) * (1 - z_bits[b] if (dz >> b) & 1 else z_bits[b])
        return index

    z_peers = [flipped(dz, 0, 0) for dz in range(zs)]
    y_peer = flipped(0, 1, 0)
    core_peer = flipped(0, 0, 1)
    after = lax.rem(me + 1, experts)
    before = lax.rem(me + experts - 1, experts)

    barrier = pltpu.get_barrier_semaphore()
    greeted = z_peers[1:] + [y_peer, core_peer, after, before]
    for peer in greeted:
        pl.semaphore_signal(barrier, inc=1, device_id={"expert": peer}, device_id_type=MESH)

    w_copies = [
        pltpu.make_async_copy(gate_hbm.at[0], gate_w, w_sem.at[0]),
        pltpu.make_async_copy(up_hbm.at[0], up_w, w_sem.at[1]),
        pltpu.make_async_copy(down_hbm.at[0], down_w, w_sem.at[2]),
    ]
    small_copies = [
        pltpu.make_async_copy(hidden_hbm, hidden_ref, w_sem.at[3]),
        pltpu.make_async_copy(ids_hbm, ids_ref, w_sem.at[4]),
        pltpu.make_async_copy(weight_hbm, weight_ref, w_sem.at[5]),
        pltpu.make_async_copy(gain_hbm, gain_ref, w_sem.at[6]),
    ]
    for copy in small_copies + w_copies:
        copy.start()

    for copy in small_copies:
        copy.wait()

    own = hidden_ref[...].astype(jnp.float32)
    scale = lax.rsqrt(jnp.mean(own * own, axis=-1, keepdims=True) + 1e-06)
    normed = (own * scale * gain_ref[...]).astype(jnp.bfloat16)
    row_no = lax.broadcasted_iota(jnp.int32, (rows, LANES), 0)
    lane = lax.broadcasted_iota(jnp.int32, (rows, LANES), 1)
    parents = jnp.zeros((rows, LANES), jnp.int32)
    for r in range(rows):
        parents = jnp.where(row_no == r, parent_ref[r], parents)
    weights = weight_ref[...].T
    share = weights / jnp.sum(weights, axis=-1, keepdims=True)
    ids = ids_ref[...].T
    spread = jnp.zeros((rows, LANES), jnp.float32)
    lane_expert = lane & (experts - 1)
    for k in range(ids.shape[1]):
        spread = spread + jnp.where(lane_expert == ids[:, k:k + 1], share[:, k:k + 1], 0.0)
    high = spread.astype(jnp.bfloat16).astype(jnp.float32)
    middle = (spread - high).astype(jnp.bfloat16).astype(jnp.float32)
    low = spread - high - middle
    meta = jnp.where(
        lane < experts, high,
        jnp.where(lane < 2 * experts, middle,
                  jnp.where(lane < 3 * experts, low,
                            jnp.where(lane == 3 * experts, parents.astype(jnp.float32), 0.0))))
    for k in range(gc):
        rows_in[k][0:rows, 0:gw] = normed[:, k * gw:(k + 1) * gw]
    rows_in[0][0:rows, gw:gw + LANES] = meta.astype(jnp.bfloat16)

    pl.semaphore_wait(barrier, len(greeted))

    sends = []

    def remote(src, dst, send, recv, peer):
        return pltpu.make_async_remote_copy(
            src_ref=src, dst_ref=dst, send_sem=send, recv_sem=recv,
            device_id={"expert": peer}, device_id_type=MESH)

    def gather(k, source, target, peer):
        buf = rows_in[k]
        return remote(buf.at[pl.ds(source * rows, rows), :], buf.at[pl.ds(target * rows, rows), :],
                      g_send.at[k, target], g_recv.at[k, target], peer)

    def go(copy):
        copy.start()
        sends.append(copy)
        return copy

    z_copies, y_copies, c_copies = [], [], []
    for k in range(gc):
        z_copies.append([None] + [go(gather(k, 0, dz, z_peers[dz])) for dz in range(1, zs)])
        y_copies.append([go(gather(k, 0, zs, y_peer))])
        c_copies.append([go(gather(k, 0, 2 * zs, core_peer))])
    before_copy = None
    tile = 256
    for stage, k, dz in gather_order(gc, zs):
        if stage == "z":
            z_copies[k][dz].wait_recv()
            y_copies[k].append(go(gather(k, dz, zs + dz, y_peer)))
            c_copies[k].append(go(gather(k, dz, 2 * zs + dz, core_peer)))
        elif stage == "y":
            y_copies[k][dz].wait_recv()
            c_copies[k].append(go(gather(k, zs + dz, 3 * zs + dz, core_peer)))
        else:
            for copy in c_copies[k]:
                copy.wait_recv()
            if k == 0:
                w_copies[0].wait()
                w_copies[1].wait()
            if k == gc - 1:
                before_copy = go(remote(hidden_ref, prev, p_sem.at[0], p_sem.at[1], after))

            @pl.loop(0, hidden_units // tile, unroll=True)
            def _(t):
                columns = pl.ds(pl.multiple_of(t * tile, tile), tile)
                block = rows_in[k][:, 0:gw]
                gate = jnp.dot(block, gate_w[k * gw:(k + 1) * gw, columns],
                               preferred_element_type=jnp.float32)
                up = jnp.dot(block, up_w[k * gw:(k + 1) * gw, columns],
                             preferred_element_type=jnp.float32)
                if k > 0:
                    gate = gate + gate_acc[:, columns]
                    up = up + up_acc[:, columns]
                if k < gc - 1:
                    gate_acc[:, columns] = gate
                    up_acc[:, columns] = up
                else:
                    inner[:, columns] = (gate / (1.0 + jnp.exp(-gate)) * up).astype(jnp.bfloat16)

            if k == 0:
                facts = rows_in[0][:, gw:gw + LANES].astype(jnp.float32)
                lanes = lax.broadcasted_iota(jnp.int32, (total, LANES), 1)
                mine = ((lanes & (experts - 1)) == me) & (lanes < 3 * experts)
                share_ref[...] = jnp.sum(jnp.where(mine, facts, 0.0), axis=1, keepdims=True)
                wanted = facts[:, 3 * experts:3 * experts + 1]
                held = lax.broadcasted_iota(jnp.int32, (8, total), 1)
                slot = held >> row_bits
                dz = slot & (zs - 1)
                dy = (slot >> bits) & 1
                dc = slot >> (bits + 1)
                owner = dc + core - 2 * core * dc + 2 * (dy + y - 2 * y * dy)
                for b in range(bits):
                    bit = (dz >> b) & 1
                    owner = owner + (4 << b) * (bit + z_bits[b] - 2 * z_bits[b] * bit)
                at = ((owner << row_bits) + (held & (rows - 1))).astype(jnp.float32)[0:1]
                choose = jnp.where(at == wanted, 1.0, 0.0).astype(jnp.bfloat16)

    forked_inner[...] = jnp.dot(
        choose, inner[...], preferred_element_type=jnp.float32).astype(jnp.bfloat16)
    w_copies[2].wait()
    core_copies = []
    for k in range(rc):

        @pl.loop(0, rw // tile, unroll=True)
        def _(t):
            columns = pl.ds(pl.multiple_of(k * rw + t * tile, tile), tile)
            local = pl.ds(pl.multiple_of(t * tile, tile), tile)
            result = jnp.dot(forked_inner[...], down_w[:, columns],
                             preferred_element_type=jnp.float32)
            result = result.astype(jnp.bfloat16).astype(jnp.float32) * share_ref[...]
            kept[k, :, local] = result[0:half]
            core_out[k, :, local] = result[half:total].astype(jnp.bfloat16)

        core_copies.append([
            go(remote(core_out.at[k, pl.ds(first, quarter)], core_in.at[k, pl.ds(first, quarter)],
                      r_send.at[k, number], r_recv.at[k, number], core_peer))
            for first, number in ((quarter, 0), (0, 2 * zs))])

    y_back = []
    for k in range(rc):
        core_copies[k][0].wait_recv()
        y_back.append([None] * zs)
        for dz in reversed(range(zs)):
            here = pl.ds(dz * rows, rows)
            there = slice(quarter + dz * rows, quarter + (dz + 1) * rows)
            y_out[k, here] = (kept[k, there] + core_in[k, there].astype(jnp.float32)
                              ).astype(jnp.bfloat16)
            y_back[k][dz] = go(remote(y_out.at[k, here], y_in.at[k, here],
                                      r_send.at[k, 1 + dz], r_recv.at[k, 1 + dz], y_peer))

    before_copy.wait_recv()
    pool_no = lax.broadcasted_iota(jnp.int32, (rows, 2 * rows), 1)
    pick = jnp.where(parents[:, 0:2 * rows] - (me - 1) * rows == pool_no, 1.0, 0.0)
    pick = pick.astype(jnp.bfloat16)

    forked = []
    for k in range(rc):
        columns = slice(k * rw, (k + 1) * rw)
        forked.append(
            jnp.dot(pick[:, 0:rows], prev[:, columns], preferred_element_type=jnp.float32)
            + jnp.dot(pick[:, rows:2 * rows], hidden_ref[:, columns],
                      preferred_element_type=jnp.float32))

    z_back = []
    for k in range(rc):
        core_copies[k][1].wait_recv()
        z_back.append([None] * zs)
        for dz in reversed(range(zs)):
            y_back[k][dz].wait_recv()
            block = slice(dz * rows, (dz + 1) * rows)
            summed = (kept[k, block] + core_in[k, block].astype(jnp.float32)
                      + y_in[k, block].astype(jnp.float32))
            if dz == 0:
                kept[k, block] = summed
            else:
                place = pl.ds((dz - 1) * rows, rows)
                z_out[k, place] = summed.astype(jnp.bfloat16)
                z_back[k][dz] = go(remote(
                    z_out.at[k, place], z_in.at[k, place],
                    r_send.at[k, zs + dz], r_recv.at[k, zs + dz], z_peers[dz]))

    for k in range(rc):
        columns = slice(k * rw, (k + 1) * rw)
        mixed = kept[k, 0:rows]
        for dz in range(1, zs):
            z_back[k][dz].wait_recv()
            mixed = mixed + z_in[k, (dz - 1) * rows:dz * rows].astype(jnp.float32)
        out_ref[:, columns] = (forked[k] + mixed).astype(out_ref.dtype)

    for copy in sends:
        copy.wait_send()


def dense(hidden, parent, expert_ids, route_weight, norm_gain, w_gate, w_up, w_down):
    rows, width = hidden.shape
    experts = lax.axis_size("expert")
    zs = experts // 4
    units = w_gate.shape[2]
    top = expert_ids.shape[1]
    total = rows * experts
    gc, rc = GATHER_CHUNKS, RETURN_CHUNKS
    gw, rw = width // gc, width // rc
    bf16, f32 = jnp.bfloat16, jnp.float32
    vmem = pl.BlockSpec(memory_space=pltpu.VMEM)
    hbm = pl.BlockSpec(memory_space=pl.ANY)
    return pl.pallas_call(
        functools.partial(dense_kernel, experts=experts, zs=zs),
        out_shape=jax.ShapeDtypeStruct((rows, width), hidden.dtype),
        in_specs=[pl.BlockSpec(memory_space=pltpu.SMEM)] + [hbm] * 7,
        out_specs=vmem,
        scratch_shapes=[
            pltpu.VMEM((total, gw + (LANES if k == 0 else 0)), bf16) for k in range(gc)
        ] + [
            pltpu.VMEM((width, units), bf16),
            pltpu.VMEM((width, units), bf16),
            pltpu.VMEM((units, width), bf16),
            pltpu.VMEM((total, units), f32),
            pltpu.VMEM((total, units), f32),
            pltpu.VMEM((total, units), bf16),
            pltpu.VMEM((total, units), bf16),
            pltpu.VMEM((total, 1), f32),
            pltpu.VMEM((rows, width), bf16),
            pltpu.VMEM((rc, total // 2, rw), f32),
            pltpu.VMEM((rc, total // 2, rw), bf16),
            pltpu.VMEM((rc, total // 2, rw), bf16),
            pltpu.VMEM((rc, total // 4, rw), bf16),
            pltpu.VMEM((rc, total // 4, rw), bf16),
            pltpu.VMEM((rc, total // 4 - rows, rw), bf16),
            pltpu.VMEM((rc, total // 4 - rows, rw), bf16),
            pltpu.VMEM(hidden.shape, bf16),
            pltpu.VMEM((top, rows), jnp.int32),
            pltpu.VMEM((top, rows), f32),
            pltpu.VMEM((1, width), f32),
            pltpu.SemaphoreType.DMA((7,)),
            pltpu.SemaphoreType.DMA((gc, 4 * zs)),
            pltpu.SemaphoreType.DMA((gc, 4 * zs)),
            pltpu.SemaphoreType.DMA((rc, 2 * zs + 1)),
            pltpu.SemaphoreType.DMA((rc, 2 * zs + 1)),
            pltpu.SemaphoreType.DMA((2,)),
        ],
        compiler_params=pltpu.CompilerParams(
            collective_id=0, has_side_effects=True, vmem_limit_bytes=56 * 1024 * 1024),
    )(parent, hidden, expert_ids.T, route_weight.T, norm_gain.reshape(1, width),
      w_gate, w_up, w_down)


def shifted(shard, axis, by):
    peers = lax.axis_size(axis)
    pairs = [(i, i + by) for i in range(peers) if 0 <= i + by < peers]
    return lax.ppermute(shard, axis, pairs)


def routed(hidden, parent, expert_ids, route_weight, norm_gain, w_gate, w_up, w_down):
    row_count = hidden.shape[0]
    width = hidden.shape[1]
    route_count = expert_ids.shape[1]
    expert_count = lax.axis_size("expert")
    capacity = 2 * row_count * route_count // expert_count
    my_index = lax.axis_index("expert")
    first_row = my_index * row_count
    before = shifted(hidden, "expert", 1)
    pool = jnp.concatenate([before, hidden], axis=0)
    local_parent = parent - (first_row - row_count)
    forked = jnp.take(pool, local_parent, axis=0)
    forked_f = forked.astype(jnp.float32)
    scale_row = lax.rsqrt(jnp.mean(forked_f * forked_f, axis=-1, keepdims=True) + 1e-06)
    normed = (forked_f * scale_row * norm_gain).astype(jnp.bfloat16)
    share = route_weight / jnp.sum(route_weight, axis=-1, keepdims=True)
    flat_ids = expert_ids.reshape(-1)
    expert_range = jnp.arange(expert_count, dtype=jnp.int32)
    onehot = (flat_ids[:, None] == expert_range[None, :]).astype(jnp.int32)
    earlier = jnp.cumsum(onehot, axis=0) - onehot
    slot_no = jnp.sum(earlier * onehot, axis=1)
    target = flat_ids * capacity + slot_no
    slot_range = jnp.arange(expert_count * capacity, dtype=jnp.int32)
    placing = (target[None, :] == slot_range[:, None]).astype(jnp.bfloat16)
    repeated = jnp.repeat(normed, route_count, axis=0)
    outgoing = jnp.dot(placing, repeated, preferred_element_type=jnp.float32).astype(jnp.bfloat16)
    outgoing = outgoing.reshape(expert_count, capacity, width)
    block = lax.all_to_all(outgoing, "expert", split_axis=0, concat_axis=0, tiled=True)
    sources = block.shape[0]
    items = block.shape[1]
    inputs = block.reshape(sources * items, width)
    gate_val = jnp.dot(inputs, w_gate[0], preferred_element_type=jnp.float32)
    up_val = jnp.dot(inputs, w_up[0], preferred_element_type=jnp.float32)
    inner = (jax.nn.silu(gate_val) * up_val).astype(jnp.bfloat16)
    result = jnp.dot(inner, w_down[0], preferred_element_type=jnp.float32).astype(jnp.bfloat16)
    result = result.reshape(sources, items, width)
    returned = lax.all_to_all(result, "expert", split_axis=0, concat_axis=0, tiled=True)
    back_flat = returned.reshape(expert_count * capacity, width).astype(jnp.float32)
    target_rows = target.reshape(row_count, route_count)
    combining = jnp.sum(
        (target_rows[:, :, None] == slot_range[None, None, :]).astype(jnp.float32)
        * share[:, :, None],
        axis=1,
    )
    mixed = jnp.dot(
        combining, back_flat, precision=lax.Precision.HIGHEST, preferred_element_type=jnp.float32
    )
    return (forked_f + mixed).astype(jnp.bfloat16)


def per_device(hidden, *others):
    experts = lax.axis_size("expert")
    slots = 2 * hidden.shape[0] * others[1].shape[1]
    fits = hidden.shape[0] * experts <= min(slots, 256) and 3 * experts < LANES
    rows = hidden.shape[0]
    if fits and experts >= 8 and experts & (experts - 1) == 0 and rows & (rows - 1) == 0:
        return dense(hidden, *others)
    return routed(hidden, *others)


def solution(mesh):
    in_specs = (
        P(("parts", "expert"), None),
        P(("parts", "expert")),
        P(("parts", "expert"), None),
        P(("parts", "expert"), None),
        P(),
        P("expert", None, None),
        P("expert", None, None),
        P("expert", None, None),
    )
    out_specs = P(("parts", "expert"), None)
    return jax.shard_map(
        per_device, mesh=mesh, in_specs=in_specs, out_specs=out_specs, check_vma=False
    )
```
